32 devices in a mesh: seq: 8 (over z, x), head: 4 (over y, core).
Axes of the slice: x: 2, y: 2, z: 4, core: 2. Of those that a mesh axis runs over, the one named last changes fastest.
Arguments:
- queries: bfloat16 [4096, 64, 128], P('seq', 'head'), may hold values from -41 to 41
- keys: bfloat16 [4096, 64, 128], P('seq', 'head'), may hold values from -6 to 6
- values: bfloat16 [4096, 64, 128], P('seq', 'head'), may hold values from -6 to 6
- cotangent: bfloat16 [4096, 64, 128], P('seq', 'head'), may hold values from -6 to 6
Outputs:
- normed_out: bfloat16 [4096, 64, 128], P('seq', 'head')
- grad_queries: bfloat16 [4096, 64, 128], P('seq', 'head')
- grad_keys: bfloat16 [4096, 64, 128], P('seq', 'head')
- grad_values: bfloat16 [4096, 64, 128], P('seq', 'head')
The draws below stay inside these ranges and needn't reach their ends.
All inputs are finite; a program needn't handle non-finite values.
Results may differ from the reference program's by a relative error of at most 0.0058.
Values sent between devices are 32-bit elements; how exact they have to be, the bound alone decides.
A program may use at most 128 MiB of HBM per device.

```python
import math
import jax
import jax.numpy as jnp
from jax import lax

HEADS = 64
DH = 128
BLK = 512
TOKENS = 4096


def draw_queries(key, part):
    streams = jax.random.split(jax.random.fold_in(key, 17), 3)
    base = jnp.clip(jax.random.normal(streams[0], (TOKENS, HEADS, DH), jnp.float32), -4.0, 4.0)
    row_span = math.log(10.0)
    head_place = (jnp.arange(HEADS, dtype=jnp.float32) + jax.random.uniform(streams[1], (HEADS,), jnp.float32)) / HEADS
    head_scale = jnp.exp(math.log(10.0) * (head_place - 0.5))
    row_scale = jnp.exp(row_span * (jax.random.uniform(streams[2], (TOKENS, 1, 1), jnp.float32) - 0.5))
    return (base * head_scale[None, :, None] * row_scale).astype(jnp.bfloat16)


def steps_of(own_key, dims, cuts, low, high):
    loudness, own = 1.0, jax.random.fold_in(own_key, 6)
    for axis_at, parts in cuts:
        steps = jnp.exp(jax.random.uniform(jax.random.fold_in(own, axis_at), (parts,), jnp.float32, low / len(cuts), high / len(cuts)))
        loudness = loudness * jnp.repeat(steps, dims[axis_at] // parts).reshape([-1 if axis == axis_at else 1 for axis in range(len(dims))])
    return loudness


def centred(stream_key, shape, spread, bound, cuts=(), held_as=jnp.bfloat16):
    entries = jax.random.normal(stream_key, shape, jnp.float32) * spread
    if len(cuts) > 0:
        entries = steps_of(stream_key, shape, cuts, -0.22, 0.18) * entries
    return jnp.clip(entries, min=-bound, max=bound).astype(held_as)


def setup_inputs(seed: int = 0) -> dict:
    splits = jax.random.split(jax.random.key(seed), 5)
    return {
        "queries": draw_queries(jax.random.fold_in(splits[4], 71), 0),
        "keys": centred(splits[1], (TOKENS, HEADS, DH), 1.0, 6.0, ((0, 8), (1, 4))),
        "values": centred(splits[2], (TOKENS, HEADS, DH), 1.0, 6.0, ((0, 8), (1, 4))),
        "cotangent": centred(splits[3], (TOKENS, HEADS, DH), 1.0, 6.0, ((0, 8), (1, 4))),
    }


EPSILON = 1e-06

def outer_sum(pair):
    left, right = pair
    return jnp.einsum('thi,thj->hij', left.astype(jnp.float32), right.astype(jnp.float32))

def low_copy(array):
    return lax.optimization_barrier(array.astype(jnp.bfloat16))

def reference(queries, keys, values, cotangent):
    count = TOKENS // BLK
    shape4 = (count, BLK, HEADS, DH)
    q_blocks = queries.reshape(shape4)
    k_blocks = keys.reshape(shape4)
    v_blocks = values.reshape(shape4)
    c_blocks = cotangent.reshape(shape4)
    kv_state = lax.map(outer_sum, (k_blocks, v_blocks))
    zero_state = jnp.zeros((1, HEADS, DH, DH), jnp.float32)
    prefix = jnp.concatenate([zero_state, jnp.cumsum(kv_state, axis=0)[:-1]], axis=0)
    state_low = low_copy(prefix)
    causal = jnp.arange(BLK)[:, None] >= jnp.arange(BLK)[None, :]

    def forward_block(items):
        q_blk, k_blk, v_blk, s_blk = items
        scores = jnp.einsum('thd,shd->hts', q_blk.astype(jnp.float32), k_blk.astype(jnp.float32))
        weights = low_copy(jnp.where(causal[None], scores, 0.0))
        local = jnp.einsum('hts,shd->thd', weights.astype(jnp.float32), v_blk.astype(jnp.float32))
        carried = jnp.einsum('thi,hij->thj', q_blk.astype(jnp.float32), s_blk.astype(jnp.float32))
        return local + carried
    raw_out = lax.map(forward_block, (q_blocks, k_blocks, v_blocks, state_low))
    mean_sq = lax.optimization_barrier(jnp.mean(raw_out * raw_out, axis=(2, 3)))
    inv_rms = lax.rsqrt(mean_sq + EPSILON)[..., None, None]
    normed_out = (raw_out * inv_rms).astype(jnp.bfloat16)
    cot_float = c_blocks.astype(jnp.float32)
    slope = lax.optimization_barrier(jnp.mean(cot_float * raw_out, axis=(2, 3)))[..., None, None] * inv_rms
    grad_raw = low_copy(inv_rms * (cot_float - raw_out * inv_rms * slope))
    qg_state = lax.map(outer_sum, (q_blocks, grad_raw))
    reverse_sum = jnp.cumsum(qg_state[::-1], axis=0)[::-1]
    suffix_low = low_copy(jnp.concatenate([reverse_sum[1:], zero_state], axis=0))

    def backward_block(items):
        q_blk, k_blk, v_blk, g_blk, s_blk, u_blk = items
        qf = q_blk.astype(jnp.float32)
        kf = k_blk.astype(jnp.float32)
        vf = v_blk.astype(jnp.float32)
        gf = g_blk.astype(jnp.float32)
        sf = s_blk.astype(jnp.float32)
        uf = u_blk.astype(jnp.float32)
        scores = jnp.einsum('thd,shd->hts', qf, kf)
        weights = low_copy(jnp.where(causal[None], scores, 0.0)).astype(jnp.float32)
        gscores = jnp.einsum('thj,shj->hts', gf, vf)
        gweights = low_copy(jnp.where(causal[None], gscores, 0.0)).astype(jnp.float32)
        grad_q = jnp.einsum('hts,shi->thi', gweights, kf) + jnp.einsum('thj,hij->thi', gf, sf)
        grad_k = jnp.einsum('hts,thi->shi', gweights, qf) + jnp.einsum('shj,hij->shi', vf, uf)
        grad_v = jnp.einsum('hts,thj->shj', weights, gf) + jnp.einsum('shi,hij->shj', kf, uf)
        return (grad_q.astype(jnp.bfloat16), grad_k.astype(jnp.bfloat16), grad_v.astype(jnp.bfloat16))
    grad_q, grad_k, grad_v = lax.map(backward_block, (q_blocks, k_blocks, v_blocks, grad_raw, state_low, suffix_low))
    full = (TOKENS, HEADS, DH)
    return (normed_out.reshape(full), grad_q.reshape(full), grad_k.reshape(full), grad_v.reshape(full))
```

```python
import functools

import jax
import jax.numpy as jnp
from jax import lax
from jax.experimental import pallas as pl
from jax.experimental.pallas import tpu as pltpu
from jax.sharding import PartitionSpec as P

EPSILON = 1e-06
CUT = 256
PARTS = 4
F32 = jnp.float32
BF16 = jnp.bfloat16
MESH = pl.DeviceIdType.MESH


def dot(a, b):
    return lax.dot_general(a, b, (((1,), (0,)), ((), ())), preferred_element_type=F32)


def dot_nt(a, b):
    return lax.dot_general(a, b, (((1,), (1,)), ((), ())), preferred_element_type=F32)


def dot_tn(a, b):
    return lax.dot_general(a, b, (((0,), (0,)), ((), ())), preferred_element_type=F32)


def kernel(n, nh, heads, toks, dim,
           q_hbm, k_hbm, v_hbm, c_hbm, no_hbm, gq_hbm, gk_hbm, gv_hbm,
           io, st0, st1, st2, st3, qh, kh, vh, ch, raw, gr,
           own, rs, rp, rx, sp, sx, low, acc, ex_send, ex_recv,
           in_sem, out_sem, rs_s, rs_r, rp_s, rp_r, rx_s, rx_r, ex_s, ex_r):
    half = heads // 2
    pairs = n // 2
    rows = toks * heads
    width = heads * nh * dim
    stages = (st0, st1, st2, st3)
    outs = (no_hbm, gq_hbm, gk_hbm, gv_hbm)
    seq = lax.axis_index("seq")
    me = lax.axis_index("head")
    pair = seq // 2
    side = seq % 2
    partner = seq + 1 - 2 * side
    own_base = side * half
    oth_base = (1 - side) * half

    loads = [
        pltpu.make_async_copy(src, io.at[a], in_sem.at[a])
        for a, src in enumerate((k_hbm, v_hbm, q_hbm, c_hbm))
    ]
    for load in loads:
        load.start()

    barrier = pltpu.get_barrier_semaphore()
    pl.semaphore_signal(barrier, inc=1, device_id={"seq": partner}, device_id_type=MESH)

    @pl.when(pair > 0)
    def _():
        pl.semaphore_signal(barrier, inc=1, device_id={"seq": (seq + n - 2) % n}, device_id_type=MESH)

    @pl.when(pair < pairs - 1)
    def _():
        pl.semaphore_signal(barrier, inc=1, device_id={"seq": (seq + 2) % n}, device_id_type=MESH)

    for d in range(1, nh):
        pl.semaphore_signal(barrier, inc=1, device_id={"head": (me + d) % nh}, device_id_type=MESH)

    def strided(ref, h):
        return ref.at[pl.ds(h, toks, stride=heads), :]

    chunk = rows // 16

    def widen(a):
        def body(j, _):
            at = pl.ds(pl.multiple_of(j * chunk, chunk), chunk)
            stages[a][at, :] = io[a, at, :].astype(F32)
            return 0
        lax.fori_loop(0, 16, body, 0)

    def store_copy(a, j):
        part = rows // PARTS
        at = pl.ds(j * part, part)
        return pltpu.make_async_copy(io.at[a, at], outs[a].at[at], out_sem.at[a, j])

    def narrow(a):
        for j in range(PARTS):
            def body(t, _, j=j):
                at = pl.ds(pl.multiple_of((j * (16 // PARTS) + t) * chunk, chunk), chunk)
                io[a, at, :] = stages[a][at, :].astype(BF16)
                return 0
            lax.fori_loop(0, 16 // PARTS, body, 0)
            store_copy(a, j).start()

    def swap(ph, c):
        return pltpu.make_async_remote_copy(
            src_ref=own.at[ph, oth_base + c], dst_ref=rs.at[ph, c],
            send_sem=rs_s.at[ph, c], recv_sem=rs_r.at[ph, c],
            device_id={"seq": partner}, device_id_type=MESH)

    def chain(ph, c):
        nxt = (seq + 2) % n if ph == 0 else (seq + n - 2) % n
        return pltpu.make_async_remote_copy(
            src_ref=sp.at[ph, c], dst_ref=rp.at[ph, c],
            send_sem=rp_s.at[ph, c], recv_sem=rp_r.at[ph, c],
            device_id={"seq": nxt}, device_id_type=MESH)

    def hand(ph, c):
        return pltpu.make_async_remote_copy(
            src_ref=sx.at[ph, c], dst_ref=rx.at[ph, c],
            send_sem=rx_s.at[ph, c], recv_sem=rx_r.at[ph, c],
            device_id={"seq": partner}, device_id_type=MESH)

    def place(ph):
        return pair if ph == 0 else pairs - 1 - pair

    def relay(ph, c):
        at = place(ph)
        later = (side == 1) if ph == 0 else (side == 0)
        swap(ph, c).wait_recv()
        mine = own[ph, own_base + c]
        theirs = rs[ph, c]

        @pl.when(at > 0)
        def _():
            chain(ph, c).wait_recv()

        so_far = rp[ph, c]

        @pl.when(at < pairs - 1)
        def _():
            sp[ph, c] = so_far + (mine + theirs)
            chain(ph, c).start()

        sx[ph, c] = so_far + jnp.where(later, 0.0, mine)
        hand(ph, c).start()
        low[ph, own_base + c] = (so_far + jnp.where(later, theirs, 0.0)).astype(BF16)

    def take(ph, c):
        hand(ph, c).wait_recv()
        low[ph, oth_base + c] = rx[ph, c].astype(BF16)

    def scan(ph, unit, finish, after_units):
        at = place(ph)

        def done_units(c):
            return jnp.where(c < 0, 0, jnp.minimum(heads, 2 * (c + 1) + 5 * at))

        def done_takes(c):
            lag = 2 + 2 * (pairs - 1 - at)
            return jnp.clip(c + 1 - lag, 0, half)

        def slot(c, _):
            def one(u, _):
                unit(jnp.where(u % 2 == 0, own_base, oth_base) + u // 2)
                return 0
            lax.fori_loop(done_units(c - 1), done_units(c), one, 0)
            if after_units is not None:
                @pl.when((done_units(c) == heads) & (done_units(c - 1) < heads))
                def _():
                    after_units()
            relay(ph, c)
            finish(own_base + c)
            lax.fori_loop(done_takes(c - 1), done_takes(c), take_one, 0)
            return 0

        def take_one(c, _):
            take(ph, c)
            finish(oth_base + c)
            return 0

        lax.fori_loop(0, half, slot, 0)
        lax.fori_loop(done_takes(half - 1), half, take_one, 0)

    for ph in range(2):
        @pl.when(place(ph) == 0)
        def _():
            rp[ph] = jnp.zeros(rp.shape[1:], F32)

    acc[...] = jnp.zeros(acc.shape, F32)
    loads[0].wait()
    widen(0)
    loads[1].wait()
    widen(1)
    pl.semaphore_wait(
        barrier, nh + jnp.where(pair > 0, 1, 0) + jnp.where(pair < pairs - 1, 1, 0))

    def kv_state(h):
        k = strided(st0, h)[...].astype(BF16)
        v = strided(st1, h)[...].astype(BF16)
        kh[h] = k
        vh[h] = v
        own[0, h] = dot_tn(k, v)

    def kv_other(c, _):
        kv_state(oth_base + c)
        swap(0, c).start()
        return 0

    def kv_own(c, _):
        kv_state(own_base + c)
        return 0

    lax.fori_loop(0, half, kv_other, 0)
    lax.fori_loop(0, half, kv_own, 0)
    loads[2].wait()
    widen(2)
    loads[3].wait()
    widen(3)

    def split_qc(h, _):
        qh[h] = strided(st2, h)[...].astype(BF16)
        ch[h] = strided(st3, h)[...].astype(BF16)
        return 0

    lax.fori_loop(0, heads, split_qc, 0)

    rest = toks - CUT

    def below(shape, shift):
        return (lax.broadcasted_iota(jnp.int32, shape, 1)
                <= lax.broadcasted_iota(jnp.int32, shape, 0) + shift)

    def above(shape):
        return (lax.broadcasted_iota(jnp.int32, shape, 1)
                >= lax.broadcasted_iota(jnp.int32, shape, 0))

    def keep(mask, x):
        return jnp.where(mask, x, 0.0).astype(BF16)

    def lower(a, b, c):
        w0 = keep(below((CUT, CUT), 0), dot_nt(a[:CUT], b[:CUT]))
        w1 = keep(below((rest, toks), CUT), dot_nt(a[CUT:], b))
        return dot(w0, c[:CUT]), dot(w1, c)

    def upper(a, b, c):
        w0 = keep(above((CUT, toks)), dot_nt(a[:CUT], b))
        w1 = keep(above((rest, rest)), dot_nt(a[CUT:], b[CUT:]))
        return dot(w0, c), dot(w1, c[CUT:])

    def local_out(h):
        first, second = lower(qh[h], kh[h], vh[h])
        raw[h, :CUT] = first
        raw[h, CUT:] = second

    def finish_out(h):
        r = raw[h] + dot(qh[h], low[0, h])
        raw[h] = r
        acc[0] += r * r
        acc[1] += ch[h].astype(F32) * r

    scan(0, local_out, finish_out, None)

    sq = jnp.sum(acc[0].T, axis=0, keepdims=True)
    inner = jnp.sum(acc[1].T, axis=0, keepdims=True)
    row = lax.broadcasted_iota(jnp.int32, (8, toks), 0)
    ex_send[...] = jnp.where(row < 4, jnp.broadcast_to(sq, (8, toks)), jnp.broadcast_to(inner, (8, toks)))
    peers = [
        pltpu.make_async_remote_copy(
            src_ref=ex_send, dst_ref=ex_recv.at[d - 1],
            send_sem=ex_s.at[d - 1], recv_sem=ex_r.at[d - 1],
            device_id={"head": (me + d) % nh}, device_id_type=MESH)
        for d in range(1, nh)
    ]
    for peer in peers:
        peer.start()
    total = ex_send[...]
    for d, peer in enumerate(peers):
        peer.wait_recv()
        total = total + ex_recv[d]
    inv = lax.rsqrt(total[0:1] / width + EPSILON)
    slope = inv * (total[4:5] / width)
    acc[0] = jnp.broadcast_to(inv, (dim, toks)).T
    acc[1] = jnp.broadcast_to(inv * slope, (dim, toks)).T

    def qg_state(h):
        g = (acc[0] * (ch[h].astype(F32) - raw[h] * acc[1])).astype(BF16)
        gr[h] = g
        own[1, h] = dot_tn(qh[h], g)

    def qg_other(c, _):
        qg_state(oth_base + c)
        swap(1, c).start()
        return 0

    def qg_own(c, _):
        qg_state(own_base + c)
        return 0

    lax.fori_loop(0, half, qg_other, 0)
    lax.fori_loop(0, half, qg_own, 0)

    def local_grads(h):
        q, k, v, g = qh[h], kh[h], vh[h], gr[h]
        strided(st0, h)[...] = raw[h] * acc[0]
        first, second = lower(g, v, k)
        strided(st1, h)[...] = jnp.concatenate([first, second], axis=0) + dot_nt(g, low[0, h])
        first, second = upper(v, g, q)
        strided(st2, h)[...] = jnp.concatenate([first, second], axis=0)
        first, second = upper(k, q, g)
        strided(st3, h)[...] = jnp.concatenate([first, second], axis=0)

    def early_outs():
        narrow(0)
        narrow(1)

    def finish_grads(h):
        strided(st2, h)[...] = strided(st2, h)[...] + dot_nt(vh[h], low[1, h])
        strided(st3, h)[...] = strided(st3, h)[...] + dot(kh[h], low[1, h])

    scan(1, local_grads, finish_grads, early_outs)
    narrow(2)
    narrow(3)

    for peer in peers:
        peer.wait_send()
    for ph in range(2):
        def drain(c, _, ph=ph):
            swap(ph, c).wait_send()
            hand(ph, c).wait_send()

            @pl.when(place(ph) < pairs - 1)
            def _():
                chain(ph, c).wait_send()
            return 0
        lax.fori_loop(0, half, drain, 0)
    for a in range(4):
        for j in range(PARTS):
            store_copy(a, j).wait()


def local(n, nh, queries, keys, values, cotangent):
    toks, heads, dim = queries.shape
    rows = toks * heads
    half = heads // 2
    flat = [x.reshape(rows, dim) for x in (queries, keys, values, cotangent)]
    any_spec = pl.BlockSpec(memory_space=pl.ANY)
    sems = pltpu.SemaphoreType.DMA
    per_head = pltpu.VMEM((heads, toks, dim), BF16)
    part = pltpu.VMEM((2, half, dim, dim), F32)
    outs = pl.pallas_call(
        functools.partial(kernel, n, nh, heads, toks, dim),
        out_shape=[jax.ShapeDtypeStruct((rows, dim), BF16)] * 4,
        in_specs=[any_spec] * 4,
        out_specs=[any_spec] * 4,
        scratch_shapes=[
            pltpu.VMEM((4, rows, dim), BF16),
            *[pltpu.VMEM((rows, dim), F32)] * 4,
            *[per_head] * 4,
            pltpu.VMEM((heads, toks, dim), F32),
            per_head,
            pltpu.VMEM((2, heads, dim, dim), F32),
            *[part] * 5,
            pltpu.VMEM((2, heads, dim, dim), BF16),
            pltpu.VMEM((2, toks, dim), F32),
            pltpu.VMEM((8, toks), F32),
            pltpu.VMEM((nh - 1, 8, toks), F32),
            sems((4,)),
            sems((4, PARTS)),
            *[sems((2, half))] * 6,
            sems((nh - 1,)),
            sems((nh - 1,)),
        ],
        compiler_params=pltpu.CompilerParams(
            collective_id=0, has_side_effects=True, vmem_limit_bytes=60 * 2**20),
        cost_estimate=pl.CostEstimate(
            flops=heads * 10 * toks * toks * dim, bytes_accessed=16 * rows * dim, transcendentals=toks),
    )(*flat)
    return tuple(x.reshape(toks, heads, dim) for x in outs)


def solution(mesh):
    n, nh = mesh.shape["seq"], mesh.shape["head"]
    spec = P("seq", "head", None)
    return jax.shard_map(
        functools.partial(local, n, nh),
        mesh=mesh,
        in_specs=(spec,) * 4,
        out_specs=(spec,) * 4,
        check_vma=False,
    )
```

```python
import functools

import jax
import jax.numpy as jnp
from jax import lax
from jax.experimental import pallas as pl
from jax.experimental.pallas import tpu as pltpu
from jax.sharding import PartitionSpec as P

EPSILON = 1e-06
CUT = 256
PARTS = 4
F32 = jnp.float32
BF16 = jnp.bfloat16
MESH = pl.DeviceIdType.MESH


def dot(a, b):
    return lax.dot_general(a, b, (((1,), (0,)), ((), ())), preferred_element_type=F32)


def dot_nt(a, b):
    return lax.dot_general(a, b, (((1,), (1,)), ((), ())), preferred_element_type=F32)


def dot_tn(a, b):
    return lax.dot_general(a, b, (((0,), (0,)), ((), ())), preferred_element_type=F32)


def kernel(n, nh, heads, toks, dim,
           q_hbm, k_hbm, v_hbm, c_hbm, no_ref, gq_ref, gk_ref, gv_ref,
           io, st0, st1, qh, kh, vh, ch, raw, gvp, gr,
           own, rs, rp, rx, sp, sx, low, acc, ex_send, ex_recv,
           in_sem, rs_s, rs_r, rp_s, rp_r, rx_s, rx_r, ex_s, ex_r):
    half = heads // 2
    pairs = n // 2
    rows = toks * heads
    width = heads * nh * dim
    seq = lax.axis_index("seq")
    me = lax.axis_index("head")
    pair = seq // 2
    side = seq % 2
    partner = seq + 1 - 2 * side
    own_base = side * half
    oth_base = (1 - side) * half

    landing = (no_ref, gq_ref, io.at[0], io.at[1])
    stages = (st0, st1, gk_ref, gv_ref)
    loads = [
        pltpu.make_async_copy(src, landing[a], in_sem.at[a])
        for a, src in enumerate((k_hbm, v_hbm, q_hbm, c_hbm))
    ]
    for load in loads:
        load.start()

    barrier = pltpu.get_barrier_semaphore()
    pl.semaphore_signal(barrier, inc=1, device_id={"seq": partner}, device_id_type=MESH)

    @pl.when(pair > 0)
    def _():
        pl.semaphore_signal(barrier, inc=1, device_id={"seq": (seq + n - 2) % n}, device_id_type=MESH)

    @pl.when(pair < pairs - 1)
    def _():
        pl.semaphore_signal(barrier, inc=1, device_id={"seq": (seq + 2) % n}, device_id_type=MESH)

    for d in range(1, nh):
        pl.semaphore_signal(barrier, inc=1, device_id={"head": (me + d) % nh}, device_id_type=MESH)

    def strided(ref, h):
        return ref.at[pl.ds(h, toks, stride=heads), :]

    chunk = rows // 16

    def widen(a):
        def body(j, _):
            at = pl.ds(pl.multiple_of(j * chunk, chunk), chunk)
            stages[a][at, :] = landing[a][at, :].astype(F32)
            return 0
        lax.fori_loop(0, 16, body, 0)

    def narrow(stage, out):
        def body(j, _):
            at = pl.ds(pl.multiple_of(j * chunk, chunk), chunk)
            out[at, :] = stage[at, :].astype(BF16)
            return 0
        lax.fori_loop(0, 16, body, 0)

    def swap(ph, c):
        return pltpu.make_async_remote_copy(
            src_ref=own.at[ph, oth_base + c], dst_ref=rs.at[ph, c],
            send_sem=rs_s.at[ph, c], recv_sem=rs_r.at[ph, c],
            device_id={"seq": partner}, device_id_type=MESH)

    def chain(ph, c):
        nxt = (seq + 2) % n if ph == 0 else (seq + n - 2) % n
        return pltpu.make_async_remote_copy(
            src_ref=sp.at[ph, c], dst_ref=rp.at[ph, c],
            send_sem=rp_s.at[ph, c], recv_sem=rp_r.at[ph, c],
            device_id={"seq": nxt}, device_id_type=MESH)

    def hand(ph, c):
        return pltpu.make_async_remote_copy(
            src_ref=sx.at[ph, c], dst_ref=rx.at[ph, c],
            send_sem=rx_s.at[ph, c], recv_sem=rx_r.at[ph, c],
            device_id={"seq": partner}, device_id_type=MESH)

    def place(ph):
        return pair if ph == 0 else pairs - 1 - pair

    def relay(ph, c):
        at = place(ph)
        later = (side == 1) if ph == 0 else (side == 0)
        swap(ph, c).wait_recv()
        mine = own[ph, own_base + c]
        theirs = rs[ph, c]

        @pl.when(at > 0)
        def _():
            chain(ph, c).wait_recv()

        so_far = rp[ph, c]

        @pl.when(at < pairs - 1)
        def _():
            sp[ph, c] = so_far + (mine + theirs)
            chain(ph, c).start()

        sx[ph, c] = so_far + jnp.where(later, 0.0, mine)
        hand(ph, c).start()
        low[ph, own_base + c] = (so_far + jnp.where(later, theirs, 0.0)).astype(BF16)

    def take(ph, c):
        hand(ph, c).wait_recv()
        low[ph, oth_base + c] = rx[ph, c].astype(BF16)

    def scan(ph, state, before, unit, finish, after):
        at = place(ph)

        def units_by(c):
            lead = jnp.where(at == 0, 0, half * at // (2 * (pairs - 1)) + (c + 1) // 2)
            return jnp.where(c < 0, 0, jnp.minimum(half, lead))

        def others_by(c):
            return jnp.where(at == 0, jnp.minimum(half, c + 4), half)

        def owns_by(c):
            return jnp.where(c < 0, 0, jnp.maximum(c + 1, units_by(c)))

        def finished_by(c):
            return jnp.where(c < 0, 0, jnp.minimum(c + 1, units_by(c)))

        def takes_by(c):
            lag = 2 + 2 * (pairs - 1 - at)
            return jnp.clip(c + 1 - lag, 0, units_by(c))

        def run(low_end, high_end, step):
            def body(c, _):
                step(c)
                return 0
            lax.fori_loop(low_end, high_end, body, 0)

        def other(c):
            state(oth_base + c)
            swap(ph, c).start()

        def take_one(c):
            take(ph, c)
            finish(oth_base + c)

        def slot(c):
            run(others_by(c - 1), others_by(c), other)
            run(owns_by(c - 1), owns_by(c), lambda j: state(own_base + j))
            run(units_by(c - 1), units_by(c), unit)
            relay(ph, c)
            run(finished_by(c - 1), finished_by(c), lambda j: finish(own_base + j))
            run(takes_by(c - 1), takes_by(c), take_one)

        run(0, others_by(-1), other)
        before()
        run(0, half, slot)
        run(units_by(half - 1), half, unit)
        run(finished_by(half - 1), half, lambda j: finish(own_base + j))
        after()
        run(takes_by(half - 1), half, take_one)

    for ph in range(2):
        @pl.when(place(ph) == 0)
        def _():
            rp[ph] = jnp.zeros(rp.shape[1:], F32)

    acc[...] = jnp.zeros(acc.shape, F32)
    loads[0].wait()
    widen(0)
    loads[1].wait()
    widen(1)
    pl.semaphore_wait(
        barrier, nh + jnp.where(pair > 0, 1, 0) + jnp.where(pair < pairs - 1, 1, 0))

    def kv_state(h):
        k = strided(st0, h)[...].astype(BF16)
        v = strided(st1, h)[...].astype(BF16)
        kh[h] = k
        vh[h] = v
        own[0, h] = dot_tn(k, v)

    def rest_of_inputs():
        loads[2].wait()
        widen(2)
        loads[3].wait()
        widen(3)

    rest = toks - CUT

    def below(shape, shift):
        return (lax.broadcasted_iota(jnp.int32, shape, 1)
                <= lax.broadcasted_iota(jnp.int32, shape, 0) + shift)

    def above(shape):
        return (lax.broadcasted_iota(jnp.int32, shape, 1)
                >= lax.broadcasted_iota(jnp.int32, shape, 0))

    def keep(mask, x):
        return jnp.where(mask, x, 0.0).astype(BF16)

    def lower(a, b, c):
        w0 = keep(below((CUT, CUT), 0), dot_nt(a[:CUT], b[:CUT]))
        w1 = keep(below((rest, toks), CUT), dot_nt(a[CUT:], b))
        return dot(w0, c[:CUT]), dot(w1, c)

    def upper(a, b, c):
        w0 = keep(above((CUT, toks)), dot_nt(a[:CUT], b))
        w1 = keep(above((rest, rest)), dot_nt(a[CUT:], b[CUT:]))
        return dot(w0, c), dot(w1, c[CUT:])

    def local_out(j):
        for h in (own_base + j, oth_base + j):
            q = strided(gk_ref, h)[...].astype(BF16)
            qh[h] = q
            ch[h] = strided(gv_ref, h)[...].astype(BF16)
            first, second = lower(q, kh[h], vh[h])
            raw[h, :CUT] = first
            raw[h, CUT:] = second

    def finish_out(h):
        r = raw[h] + dot(qh[h], low[0, h])
        raw[h] = r
        acc[0] += r * r
        acc[1] += ch[h].astype(F32) * r

    scan(0, kv_state, rest_of_inputs, local_out, finish_out, lambda: None)

    sq = jnp.sum(acc[0].T, axis=0, keepdims=True)
    inner = jnp.sum(acc[1].T, axis=0, keepdims=True)
    row = lax.broadcasted_iota(jnp.int32, (8, toks), 0)
    ex_send[...] = jnp.where(row < 4, jnp.broadcast_to(sq, (8, toks)), jnp.broadcast_to(inner, (8, toks)))
    peers = [
        pltpu.make_async_remote_copy(
            src_ref=ex_send, dst_ref=ex_recv.at[d - 1],
            send_sem=ex_s.at[d - 1], recv_sem=ex_r.at[d - 1],
            device_id={"head": (me + d) % nh}, device_id_type=MESH)
        for d in range(1, nh)
    ]
    for peer in peers:
        peer.start()
    total = ex_send[...]
    for d, peer in enumerate(peers):
        peer.wait_recv()
        total = total + ex_recv[d]
    inv = lax.rsqrt(total[0:1] / width + EPSILON)
    slope = inv * (total[4:5] / width)
    acc[0] = jnp.broadcast_to(inv, (dim, toks)).T
    acc[1] = jnp.broadcast_to(inv * slope, (dim, toks)).T

    def qg_state(h):
        g = (acc[0] * (ch[h].astype(F32) - raw[h] * acc[1])).astype(BF16)
        gr[h] = g
        own[1, h] = dot_tn(qh[h], g)

    def local_grads(j):
        for h in (own_base + j, oth_base + j):
            q, k, v, g = qh[h], kh[h], vh[h], gr[h]
            strided(st0, h)[...] = raw[h] * acc[0]
            first, second = lower(g, v, k)
            strided(st1, h)[...] = jnp.concatenate([first, second], axis=0) + dot_nt(g, low[0, h])
            first, second = upper(v, g, q)
            raw[h, :CUT] = first
            raw[h, CUT:] = second
            first, second = upper(k, q, g)
            gvp[h, :CUT] = first
            gvp[h, CUT:] = second

    def finish_grads(h):
        strided(gk_ref, h)[...] = raw[h] + dot_nt(vh[h], low[1, h])
        strided(gv_ref, h)[...] = gvp[h] + dot(kh[h], low[1, h])

    def early_outs():
        narrow(st0, no_ref)
        narrow(st1, gq_ref)

    scan(1, qg_state, lambda: None, local_grads, finish_grads, early_outs)

    for peer in peers:
        peer.wait_send()
    for ph in range(2):
        def drain(c, _, ph=ph):
            swap(ph, c).wait_send()
            hand(ph, c).wait_send()

            @pl.when(place(ph) < pairs - 1)
            def _():
                chain(ph, c).wait_send()
            return 0
        lax.fori_loop(0, half, drain, 0)


def write_out(no_ref, gq_ref, gk_ref, gv_ref, no_hbm, gq_hbm, gk_hbm, gv_hbm, low, sem, part_sem):
    rows = no_ref.shape[0]
    part = rows // PARTS
    copies = [
        pltpu.make_async_copy(no_ref, no_hbm, sem.at[0]),
        pltpu.make_async_copy(gq_ref, gq_hbm, sem.at[1]),
    ]
    for copy in copies:
        copy.start()
    chunk = part // 4
    for a, (src, dst) in enumerate(((gk_ref, gk_hbm), (gv_ref, gv_hbm))):
        for j in range(PARTS):
            def body(t, _):
                at = pl.ds(pl.multiple_of(j * part + t * chunk, chunk), chunk)
                low[a, at, :] = src[at, :].astype(BF16)
                return 0
            lax.fori_loop(0, 4, body, 0)
            at = pl.ds(j * part, part)
            copy = pltpu.make_async_copy(low.at[a, at], dst.at[at], part_sem.at[a, j])
            copy.start()
            copies.append(copy)
    for copy in copies:
        copy.wait()


def local(n, nh, queries, keys, values, cotangent):
    toks, heads, dim = queries.shape
    rows = toks * heads
    half = heads // 2
    flat = [x.reshape(rows, dim) for x in (queries, keys, values, cotangent)]
    any_spec = pl.BlockSpec(memory_space=pl.ANY)
    sems = pltpu.SemaphoreType.DMA
    per_head = pltpu.VMEM((heads, toks, dim), BF16)
    part = pltpu.VMEM((2, half, dim, dim), F32)
    in_vmem = pl.BlockSpec(memory_space=pltpu.VMEM)
    made = pl.pallas_call(
        functools.partial(kernel, n, nh, heads, toks, dim),
        out_shape=[pltpu.VMEM((rows, dim), kind) for kind in (BF16, BF16, F32, F32)],
        in_specs=[any_spec] * 4,
        out_specs=[in_vmem] * 4,
        scratch_shapes=[
            pltpu.VMEM((2, rows, dim), BF16),
            *[pltpu.VMEM((rows, dim), F32)] * 2,
            *[per_head] * 4,
            *[pltpu.VMEM((heads, toks, dim), F32)] * 2,
            per_head,
            pltpu.VMEM((2, heads, dim, dim), F32),
            *[part] * 5,
            pltpu.VMEM((2, heads, dim, dim), BF16),
            pltpu.VMEM((2, toks, dim), F32),
            pltpu.VMEM((8, toks), F32),
            pltpu.VMEM((nh - 1, 8, toks), F32),
            sems((4,)),
            *[sems((2, half))] * 6,
            sems((nh - 1,)),
            sems((nh - 1,)),
        ],
        compiler_params=pltpu.CompilerParams(
            collective_id=0, has_side_effects=True, vmem_limit_bytes=44 * 2**20),
        cost_estimate=pl.CostEstimate(
            flops=heads * 10 * toks * toks * dim, bytes_accessed=8 * rows * dim, transcendentals=toks),
    )(*flat)
    outs = pl.pallas_call(
        write_out,
        out_shape=[jax.ShapeDtypeStruct((rows, dim), BF16)] * 4,
        in_specs=[in_vmem] * 4,
        out_specs=[any_spec] * 4,
        scratch_shapes=[pltpu.VMEM((2, rows, dim), BF16), sems((2,)), sems((2, PARTS))],
        compiler_params=pltpu.CompilerParams(vmem_limit_bytes=16 * 2**20),
        cost_estimate=pl.CostEstimate(flops=0, bytes_accessed=8 * rows * dim, transcendentals=0),
    )(*made)
    return tuple(x.reshape(toks, heads, dim) for x in outs)


def solution(mesh):
    n, nh = mesh.shape["seq"], mesh.shape["head"]
    spec = P("seq", "head", None)
    return jax.shard_map(
        functools.partial(local, n, nh),
        mesh=mesh,
        in_specs=(spec,) * 4,
        out_specs=(spec,) * 4,
        check_vma=False,
    )
```

```python
import functools

import jax
import jax.numpy as jnp
from jax import lax
from jax.experimental import pallas as pl
from jax.experimental.pallas import tpu as pltpu
from jax.sharding import PartitionSpec as P

EPSILON = 1e-06
CUT = 256
PARTS = 4
TOKS_STEP = 16
F32 = jnp.float32
BF16 = jnp.bfloat16
MESH = pl.DeviceIdType.MESH


def dot(a, b):
    return lax.dot_general(a, b, (((1,), (0,)), ((), ())), preferred_element_type=F32)


def dot_nt(a, b):
    return lax.dot_general(a, b, (((1,), (1,)), ((), ())), preferred_element_type=F32)


def dot_tn(a, b):
    return lax.dot_general(a, b, (((0,), (0,)), ((), ())), preferred_element_type=F32)


def token_rows(heads, token, group):
    return pl.ds(group * 8 * (token[1] + 1) + token[0], 8, stride=token[1] + 1)


def spread(src, dst, heads):
    toks = src.shape[0] // heads

    def body(j, _):
        start = j * TOKS_STEP
        x = src[pl.ds(pl.multiple_of(start * heads, TOKS_STEP * heads), TOKS_STEP * heads), :].astype(F32)
        for t in range(TOKS_STEP):
            for group in range(heads // 8):
                at = t * heads + group * 8
                dst[token_rows(heads, (start + t, toks), group), :] = x[at:at + 8]
        return 0
    lax.fori_loop(0, toks // TOKS_STEP, body, 0)


def gather(src, dst, heads, first, count):
    toks = dst.shape[0] // heads

    def body(j, _):
        start = first + j * TOKS_STEP
        x = jnp.concatenate([
            src[token_rows(heads, (start + t, toks), group), :]
            for t in range(TOKS_STEP) for group in range(heads // 8)
        ], axis=0)
        at = pl.ds(pl.multiple_of(start * heads, TOKS_STEP * heads), TOKS_STEP * heads)
        dst[at, :] = x.astype(BF16)
        return 0
    lax.fori_loop(0, count // TOKS_STEP, body, 0)


def kernel(n, nh, heads, toks, dim,
           q_hbm, k_hbm, v_hbm, c_hbm, no_ref, gq_ref, gk_ref, gv_ref,
           io, st0, st1, qh, kh, vh, ch, raw, gvp, gr,
           own, rs, rp, rx, sp, sx, low, acc, ex_send, ex_recv,
           in_sem, rs_s, rs_r, rp_s, rp_r, rx_s, rx_r, ex_s, ex_r):
    half = heads // 2
    pairs = n // 2
    rows = toks * heads
    width = heads * nh * dim
    seq = lax.axis_index("seq")
    me = lax.axis_index("head")
    pair = seq // 2
    side = seq % 2
    partner = seq + 1 - 2 * side
    own_base = side * half
    oth_base = (1 - side) * half

    landing = (no_ref, gq_ref, io.at[0], io.at[1])
    stages = (st0, st1, gk_ref, gv_ref)
    loads = [
        pltpu.make_async_copy(src, landing[a], in_sem.at[a])
        for a, src in enumerate((k_hbm, v_hbm, q_hbm, c_hbm))
    ]
    for load in loads:
        load.start()

    barrier = pltpu.get_barrier_semaphore()
    pl.semaphore_signal(barrier, inc=1, device_id={"seq": partner}, device_id_type=MESH)

    @pl.when(pair > 0)
    def _():
        pl.semaphore_signal(barrier, inc=1, device_id={"seq": (seq + n - 2) % n}, device_id_type=MESH)

    @pl.when(pair < pairs - 1)
    def _():
        pl.semaphore_signal(barrier, inc=1, device_id={"seq": (seq + 2) % n}, device_id_type=MESH)

    for d in range(1, nh):
        pl.semaphore_signal(barrier, inc=1, device_id={"head": (me + d) % nh}, device_id_type=MESH)

    def of_head(ref, h):
        return ref.at[pl.ds(h * (toks + 1), toks), :]

    def swap(ph, c):
        return pltpu.make_async_remote_copy(
            src_ref=own.at[ph, oth_base + c], dst_ref=rs.at[ph, c],
            send_sem=rs_s.at[ph, c], recv_sem=rs_r.at[ph, c],
            device_id={"seq": partner}, device_id_type=MESH)

    def chain(ph, c):
        nxt = (seq + 2) % n if ph == 0 else (seq + n - 2) % n
        return pltpu.make_async_remote_copy(
            src_ref=sp.at[ph, c], dst_ref=rp.at[ph, c],
            send_sem=rp_s.at[ph, c], recv_sem=rp_r.at[ph, c],
            device_id={"seq": nxt}, device_id_type=MESH)

    def hand(ph, c):
        return pltpu.make_async_remote_copy(
            src_ref=sx.at[ph, c], dst_ref=rx.at[ph, c],
            send_sem=rx_s.at[ph, c], recv_sem=rx_r.at[ph, c],
            device_id={"seq": partner}, device_id_type=MESH)

    def place(ph):
        return pair if ph == 0 else pairs - 1 - pair

    def relay(ph, c):
        at = place(ph)
        later = (side == 1) if ph == 0 else (side == 0)
        swap(ph, c).wait_recv()
        mine = own[ph, own_base + c]
        theirs = rs[ph, c]

        @pl.when(at > 0)
        def _():
            chain(ph, c).wait_recv()

        so_far = rp[ph, c]

        @pl.when(at < pairs - 1)
        def _():
            sp[ph, c] = so_far + (mine + theirs)
            chain(ph, c).start()

        sx[ph, c] = so_far + jnp.where(later, 0.0, mine)
        hand(ph, c).start()
        low[ph, own_base + c] = (so_far + jnp.where(later, theirs, 0.0)).astype(BF16)

    def take(ph, c):
        hand(ph, c).wait_recv()
        low[ph, oth_base + c] = rx[ph, c].astype(BF16)

    def scan(ph, state, before, unit, finish, after):
        at = place(ph)

        def units_by(c):
            lead = jnp.where(at == 0, (c + 1) // 3, half * at // (2 * (pairs - 1)) + (c + 1) // 2)
            return jnp.where(c < 0, 0, jnp.minimum(half, lead))

        def others_by(c):
            return jnp.where(at == 0, jnp.clip(c + 4, 0, half), half)

        def owns_by(c):
            return jnp.where(c < 0, 0, jnp.maximum(c + 1, units_by(c)))

        def finished_by(c):
            return jnp.where(c < 0, 0, jnp.minimum(c + 1, units_by(c)))

        def takes_by(c):
            lag = 2 + 2 * (pairs - 1 - at)
            return jnp.clip(c + 1 - lag, 0, units_by(c))

        def run(low_end, high_end, step):
            def body(c, _):
                step(c)
                return 0
            lax.fori_loop(low_end, high_end, body, 0)

        def other(c):
            state(oth_base + c)
            swap(ph, c).start()

        def take_one(c):
            take(ph, c)
            finish(oth_base + c)

        def slot(c):
            run(others_by(c - 1), others_by(c), other)
            run(owns_by(c - 1), owns_by(c), lambda j: state(own_base + j))
            run(units_by(c - 1), units_by(c), unit)
            relay(ph, c)
            run(finished_by(c - 1), finished_by(c), lambda j: finish(own_base + j))
            run(takes_by(c - 1), takes_by(c), take_one)

        run(0, others_by(-1), other)
        before()
        run(0, half, slot)
        run(units_by(half - 1), half, unit)
        run(finished_by(half - 1), half, lambda j: finish(own_base + j))
        after()
        run(takes_by(half - 1), half, take_one)

    for ph in range(2):
        @pl.when(place(ph) == 0)
        def _():
            rp[ph] = jnp.zeros(rp.shape[1:], F32)

    acc[...] = jnp.zeros(acc.shape, F32)
    loads[0].wait()
    spread(landing[0], stages[0], heads)
    loads[1].wait()
    spread(landing[1], stages[1], heads)
    pl.semaphore_wait(
        barrier, nh + jnp.where(pair > 0, 1, 0) + jnp.where(pair < pairs - 1, 1, 0))

    def kv_state(h):
        k = of_head(st0, h)[...].astype(BF16)
        v = of_head(st1, h)[...].astype(BF16)
        kh[h] = k
        vh[h] = v
        own[0, h] = dot_tn(k, v)

    def rest_of_inputs():
        loads[2].wait()
        spread(landing[2], stages[2], heads)
        loads[3].wait()
        spread(landing[3], stages[3], heads)

    rest = toks - CUT

    def below(shape, shift):
        return (lax.broadcasted_iota(jnp.int32, shape, 1)
                <= lax.broadcasted_iota(jnp.int32, shape, 0) + shift)

    def above(shape):
        return (lax.broadcasted_iota(jnp.int32, shape, 1)
                >= lax.broadcasted_iota(jnp.int32, shape, 0))

    def keep(mask, x):
        return jnp.where(mask, x, 0.0).astype(BF16)

    def lower(a, b, c):
        w0 = keep(below((CUT, CUT), 0), dot_nt(a[:CUT], b[:CUT]))
        w1 = keep(below((rest, toks), CUT), dot_nt(a[CUT:], b))
        return dot(w0, c[:CUT]), dot(w1, c)

    def upper(a, b, c):
        w0 = keep(above((CUT, toks)), dot_nt(a[:CUT], b))
        w1 = keep(above((rest, rest)), dot_nt(a[CUT:], b[CUT:]))
        return dot(w0, c), dot(w1, c[CUT:])

    def local_out(j):
        for h in (own_base + j, oth_base + j):
            q = of_head(gk_ref, h)[...].astype(BF16)
            qh[h] = q
            ch[h] = of_head(gv_ref, h)[...].astype(BF16)
            first, second = lower(q, kh[h], vh[h])
            raw[h, :CUT] = first
            raw[h, CUT:] = second

    def finish_out(h):
        r = raw[h] + dot(qh[h], low[0, h])
        raw[h] = r
        acc[0] += r * r
        acc[1] += ch[h].astype(F32) * r

    scan(0, kv_state, rest_of_inputs, local_out, finish_out, lambda: None)

    sq = jnp.sum(acc[0].T, axis=0, keepdims=True)
    inner = jnp.sum(acc[1].T, axis=0, keepdims=True)
    row = lax.broadcasted_iota(jnp.int32, (8, toks), 0)
    ex_send[...] = jnp.where(row < 4, jnp.broadcast_to(sq, (8, toks)), jnp.broadcast_to(inner, (8, toks)))
    peers = [
        pltpu.make_async_remote_copy(
            src_ref=ex_send, dst_ref=ex_recv.at[d - 1],
            send_sem=ex_s.at[d - 1], recv_sem=ex_r.at[d - 1],
            device_id={"head": (me + d) % nh}, device_id_type=MESH)
        for d in range(1, nh)
    ]
    for peer in peers:
        peer.start()
    total = ex_send[...]
    for d, peer in enumerate(peers):
        peer.wait_recv()
        total = total + ex_recv[d]
    inv = lax.rsqrt(total[0:1] / width + EPSILON)
    slope = inv * (total[4:5] / width)
    acc[0] = jnp.broadcast_to(inv, (dim, toks)).T
    acc[1] = jnp.broadcast_to(inv * slope, (dim, toks)).T

    def qg_state(h):
        g = (acc[0] * (ch[h].astype(F32) - raw[h] * acc[1])).astype(BF16)
        gr[h] = g
        own[1, h] = dot_tn(qh[h], g)

    def local_grads(j):
        for h in (own_base + j, oth_base + j):
            q, k, v, g = qh[h], kh[h], vh[h], gr[h]
            of_head(st0, h)[...] = raw[h] * acc[0]
            first, second = lower(g, v, k)
            of_head(st1, h)[...] = jnp.concatenate([first, second], axis=0) + dot_nt(g, low[0, h])
            first, second = upper(v, g, q)
            raw[h, :CUT] = first
            raw[h, CUT:] = second
            first, second = upper(k, q, g)
            gvp[h, :CUT] = first
            gvp[h, CUT:] = second

    def finish_grads(h):
        of_head(gk_ref, h)[...] = raw[h] + dot_nt(vh[h], low[1, h])
        of_head(gv_ref, h)[...] = gvp[h] + dot(kh[h], low[1, h])

    def early_outs():
        gather(st0, no_ref, heads, 0, toks)
        gather(st1, gq_ref, heads, 0, toks)

    scan(1, qg_state, lambda: None, local_grads, finish_grads, early_outs)

    for peer in peers:
        peer.wait_send()
    for ph in range(2):
        def drain(c, _, ph=ph):
            swap(ph, c).wait_send()
            hand(ph, c).wait_send()

            @pl.when(place(ph) < pairs - 1)
            def _():
                chain(ph, c).wait_send()
            return 0
        lax.fori_loop(0, half, drain, 0)


def write_out(heads, no_ref, gq_ref, gk_ref, gv_ref, no_hbm, gq_hbm, gk_hbm, gv_hbm,
              low_k, low_v, sem, part_sem):
    rows = no_ref.shape[0]
    part = rows // PARTS
    toks = rows // heads
    copies = [
        pltpu.make_async_copy(no_ref, no_hbm, sem.at[0]),
        pltpu.make_async_copy(gq_ref, gq_hbm, sem.at[1]),
    ]
    for copy in copies:
        copy.start()
    for a, (src, low, dst) in enumerate(((gk_ref, low_k, gk_hbm), (gv_ref, low_v, gv_hbm))):
        for j in range(PARTS):
            gather(src, low, heads, j * (toks // PARTS), toks // PARTS)
            at = pl.ds(j * part, part)
            copy = pltpu.make_async_copy(low.at[at], dst.at[at], part_sem.at[a, j])
            copy.start()
            copies.append(copy)
    for copy in copies:
        copy.wait()


def local(n, nh, queries, keys, values, cotangent):
    toks, heads, dim = queries.shape
    rows = toks * heads
    half = heads // 2
    flat = [x.reshape(rows, dim) for x in (queries, keys, values, cotangent)]
    any_spec = pl.BlockSpec(memory_space=pl.ANY)
    sems = pltpu.SemaphoreType.DMA
    per_head = pltpu.VMEM((heads, toks, dim), BF16)
    part = pltpu.VMEM((2, half, dim, dim), F32)
    in_vmem = pl.BlockSpec(memory_space=pltpu.VMEM)
    made = pl.pallas_call(
        functools.partial(kernel, n, nh, heads, toks, dim),
        out_shape=[pltpu.VMEM((rows, dim), BF16)] * 2 + [pltpu.VMEM((rows + heads, dim), F32)] * 2,
        in_specs=[any_spec] * 4,
        out_specs=[in_vmem] * 4,
        scratch_shapes=[
            pltpu.VMEM((2, rows, dim), BF16),
            *[pltpu.VMEM((rows + heads, dim), F32)] * 2,
            *[per_head] * 4,
            *[pltpu.VMEM((heads, toks, dim), F32)] * 2,
            per_head,
            pltpu.VMEM((2, heads, dim, dim), F32),
            *[part] * 5,
            pltpu.VMEM((2, heads, dim, dim), BF16),
            pltpu.VMEM((2, toks, dim), F32),
            pltpu.VMEM((8, toks), F32),
            pltpu.VMEM((nh - 1, 8, toks), F32),
            sems((4,)),
            *[sems((2, half))] * 6,
            sems((nh - 1,)),
            sems((nh - 1,)),
        ],
        compiler_params=pltpu.CompilerParams(
            collective_id=0, has_side_effects=True, vmem_limit_bytes=44 * 2**20),
        cost_estimate=pl.CostEstimate(
            flops=heads * 10 * toks * toks * dim, bytes_accessed=8 * rows * dim, transcendentals=toks),
    )(*flat)
    outs = pl.pallas_call(
        functools.partial(write_out, heads),
        out_shape=[jax.ShapeDtypeStruct((rows, dim), BF16)] * 4,
        in_specs=[in_vmem] * 4,
        out_specs=[any_spec] * 4,
        scratch_shapes=[*[pltpu.VMEM((rows, dim), BF16)] * 2, sems((2,)), sems((2, PARTS))],
        compiler_params=pltpu.CompilerParams(vmem_limit_bytes=16 * 2**20),
        cost_estimate=pl.CostEstimate(flops=0, bytes_accessed=8 * rows * dim, transcendentals=0),
    )(*made)
    return tuple(x.reshape(toks, heads, dim) for x in outs)


def solution(mesh):
    n, nh = mesh.shape["seq"], mesh.shape["head"]
    spec = P("seq", "head", None)
    return jax.shard_map(
        functools.partial(local, n, nh),
        mesh=mesh,
        in_specs=(spec,) * 4,
        out_specs=(spec,) * 4,
        check_vma=False,
    )
```

```python
import functools

import jax
import jax.numpy as jnp
from jax import lax
from jax.experimental import pallas as pl
from jax.experimental.pallas import tpu as pltpu
from jax.sharding import PartitionSpec as P

EPSILON = 1e-06
CUT = 256
PARTS = 4
TOKS_STEP = 16
F32 = jnp.float32
BF16 = jnp.bfloat16
MESH = pl.DeviceIdType.MESH


def dot(a, b):
    return lax.dot_general(a, b, (((1,), (0,)), ((), ())), preferred_element_type=F32)


def dot_nt(a, b):
    return lax.dot_general(a, b, (((1,), (1,)), ((), ())), preferred_element_type=F32)


def dot_tn(a, b):
    return lax.dot_general(a, b, (((0,), (0,)), ((), ())), preferred_element_type=F32)


def token_rows(heads, token, group):
    return pl.ds(group * 8 * (token[1] + 1) + token[0], 8, stride=token[1] + 1)


def spread(src, dst, heads):
    toks = src.shape[0] // heads

    def body(j, _):
        start = j * TOKS_STEP
        x = src[pl.ds(pl.multiple_of(start * heads, TOKS_STEP * heads), TOKS_STEP * heads), :].astype(F32)
        for t in range(TOKS_STEP):
            for group in range(heads // 8):
                at = t * heads + group * 8
                dst[token_rows(heads, (start + t, toks), group), :] = x[at:at + 8]
        return 0
    lax.fori_loop(0, toks // TOKS_STEP, body, 0)


def gather(src, dst, heads, first, count):
    toks = dst.shape[0] // heads

    def body(j, _):
        start = first + j * TOKS_STEP
        x = jnp.concatenate([
            src[token_rows(heads, (start + t, toks), group), :]
            for t in range(TOKS_STEP) for group in range(heads // 8)
        ], axis=0)
        at = pl.ds(pl.multiple_of(start * heads, TOKS_STEP * heads), TOKS_STEP * heads)
        dst[at, :] = x.astype(BF16)
        return 0
    lax.fori_loop(0, count // TOKS_STEP, body, 0)


def kernel(n, nh, heads, toks, dim,
           q_hbm, k_hbm, v_hbm, c_hbm, no_ref, gq_ref, gk_ref, gv_ref,
           io, st0, st1, qh, kh, vh, ch, raw, gvp, gr,
           own, rs, rp, rx, sp, sx, low, acc, ex_send, ex_recv,
           in_sem, rs_s, rs_r, rp_s, rp_r, rx_s, rx_r, ex_s, ex_r):
    half = heads // 2
    pairs = n // 2
    rows = toks * heads
    width = heads * nh * dim
    seq = lax.axis_index("seq")
    me = lax.axis_index("head")
    pair = seq // 2
    side = seq % 2
    partner = seq + 1 - 2 * side
    own_base = side * half
    oth_base = (1 - side) * half

    landing = (no_ref, gq_ref, io.at[0], io.at[1])
    stages = (st0, st1, gk_ref, gv_ref)
    loads = [
        pltpu.make_async_copy(src, landing[a], in_sem.at[a])
        for a, src in enumerate((k_hbm, v_hbm, q_hbm, c_hbm))
    ]
    loads[0].start()
    loads[1].start()

    barrier = pltpu.get_barrier_semaphore()
    pl.semaphore_signal(barrier, inc=1, device_id={"seq": partner}, device_id_type=MESH)

    @pl.when(pair > 0)
    def _():
        pl.semaphore_signal(barrier, inc=1, device_id={"seq": (seq + n - 2) % n}, device_id_type=MESH)

    @pl.when(pair < pairs - 1)
    def _():
        pl.semaphore_signal(barrier, inc=1, device_id={"seq": (seq + 2) % n}, device_id_type=MESH)

    for d in range(1, nh):
        pl.semaphore_signal(barrier, inc=1, device_id={"head": (me + d) % nh}, device_id_type=MESH)

    def of_head(ref, h):
        return ref.at[pl.ds(h * (toks + 1), toks), :]

    def swap(ph, c):
        return pltpu.make_async_remote_copy(
            src_ref=own.at[ph, oth_base + c], dst_ref=rs.at[ph, c],
            send_sem=rs_s.at[ph, c], recv_sem=rs_r.at[ph, c],
            device_id={"seq": partner}, device_id_type=MESH)

    def chain(ph, c):
        nxt = (seq + 2) % n if ph == 0 else (seq + n - 2) % n
        return pltpu.make_async_remote_copy(
            src_ref=sp.at[ph, c], dst_ref=rp.at[ph, c],
            send_sem=rp_s.at[ph, c], recv_sem=rp_r.at[ph, c],
            device_id={"seq": nxt}, device_id_type=MESH)

    def hand(ph, c):
        return pltpu.make_async_remote_copy(
            src_ref=sx.at[ph, c], dst_ref=rx.at[ph, c],
            send_sem=rx_s.at[ph, c], recv_sem=rx_r.at[ph, c],
            device_id={"seq": partner}, device_id_type=MESH)

    def place(ph):
        return pair if ph == 0 else pairs - 1 - pair

    def relay(ph, c):
        at = place(ph)
        later = (side == 1) if ph == 0 else (side == 0)
        swap(ph, c).wait_recv()
        mine = own[ph, own_base + c]
        theirs = rs[ph, c]

        @pl.when(at > 0)
        def _():
            chain(ph, c).wait_recv()

        so_far = rp[ph, c]

        @pl.when(at < pairs - 1)
        def _():
            sp[ph, c] = so_far + (mine + theirs)
            chain(ph, c).start()

        sx[ph, c] = so_far + jnp.where(later, 0.0, mine)
        low[ph, own_base + c] = (so_far + jnp.where(later, theirs, 0.0)).astype(BF16)

    def take(ph, c):
        hand(ph, c).wait_recv()
        low[ph, oth_base + c] = rx[ph, c].astype(BF16)

    def scan(ph, state, before, unit, finish, after):
        at = place(ph)

        def units_by(c):
            lead = half * at // (2 * (pairs - 1)) + (c + 1) * at // (pairs - 1)
            lead = jnp.where(at == 0, (c + 1) // 3, lead)
            return jnp.where(c < 0, 0, jnp.minimum(half, lead))

        def others_by(c):
            return jnp.where(at == 0, jnp.clip(c + 4, 0, half), half)

        def owns_by(c):
            return jnp.where(c < 0, 0, jnp.maximum(c + 1, units_by(c)))

        def finished_by(c):
            return jnp.where(c < 0, 0, jnp.minimum(c + 1, units_by(c)))

        defer = half * (pairs - 1 - at) // (pairs - 1)

        def hands_by(c):
            return jnp.clip(c + 1 - defer, 0, half)

        def takes_by(c):
            return jnp.clip(c - 1 - defer, 0, units_by(c))

        def run(low_end, high_end, step):
            def body(c, _):
                step(c)
                return 0
            lax.fori_loop(low_end, high_end, body, 0)

        def other(c):
            state(oth_base + c)
            swap(ph, c).start()

        def give(c):
            hand(ph, c).start()

        def take_one(c):
            take(ph, c)
            finish(oth_base + c)

        def slot(c):
            run(others_by(c - 1), others_by(c), other)
            run(owns_by(c - 1), owns_by(c), lambda j: state(own_base + j))
            run(units_by(c - 1), units_by(c), unit)
            if after is not None:
                @pl.when((units_by(c) == half) & (units_by(c - 1) < half))
                def _():
                    after()
            relay(ph, c)
            run(hands_by(c - 1), hands_by(c), give)
            run(finished_by(c - 1), finished_by(c), lambda j: finish(own_base + j))
            run(takes_by(c - 1), takes_by(c), take_one)

        run(0, others_by(-1), other)
        before()
        run(0, half, slot)
        run(hands_by(half - 1), half, give)
        run(units_by(half - 1), half, unit)
        if after is not None:
            @pl.when(units_by(half - 1) < half)
            def _():
                after()
        run(finished_by(half - 1), half, lambda j: finish(own_base + j))
        run(takes_by(half - 1), half, take_one)

    for ph in range(2):
        @pl.when(place(ph) == 0)
        def _():
            rp[ph] = jnp.zeros(rp.shape[1:], F32)

    acc[...] = jnp.zeros(acc.shape, F32)
    loads[0].wait()
    loads[2].start()
    loads[3].start()
    spread(landing[0], stages[0], heads)
    loads[1].wait()
    spread(landing[1], stages[1], heads)
    pl.semaphore_wait(
        barrier, nh + jnp.where(pair > 0, 1, 0) + jnp.where(pair < pairs - 1, 1, 0))

    def kv_state(h):
        k = of_head(st0, h)[...].astype(BF16)
        v = of_head(st1, h)[...].astype(BF16)
        kh[h] = k
        vh[h] = v
        own[0, h] = dot_tn(k, v)

    def rest_of_inputs():
        loads[2].wait()
        spread(landing[2], stages[2], heads)
        loads[3].wait()
        spread(landing[3], stages[3], heads)

    def square(compare):
        return compare(lax.broadcasted_iota(jnp.int32, (CUT, CUT), 1),
                       lax.broadcasted_iota(jnp.int32, (CUT, CUT), 0))

    def keep(mask, x):
        return jnp.where(mask, x, 0.0).astype(BF16)

    def lower(a, b, c):
        mask = square(jnp.less_equal)
        w0 = keep(mask, dot_nt(a[:CUT], b[:CUT]))
        w1 = dot_nt(a[CUT:], b)
        w1 = jnp.concatenate([w1[:, :CUT].astype(BF16), keep(mask, w1[:, CUT:])], axis=1)
        return dot(w0, c[:CUT]), dot(w1, c)

    def upper(a, b, c):
        mask = square(jnp.greater_equal)
        w0 = dot_nt(a[:CUT], b)
        w0 = jnp.concatenate([keep(mask, w0[:, :CUT]), w0[:, CUT:].astype(BF16)], axis=1)
        w1 = keep(mask, dot_nt(a[CUT:], b[CUT:]))
        return dot(w0, c), dot(w1, c[CUT:])

    def local_out(j):
        for h in (own_base + j, oth_base + j):
            q = of_head(gk_ref, h)[...].astype(BF16)
            qh[h] = q
            ch[h] = of_head(gv_ref, h)[...].astype(BF16)
            first, second = lower(q, kh[h], vh[h])
            raw[h, :CUT] = first
            raw[h, CUT:] = second

    def finish_out(h):
        r = raw[h] + dot(qh[h], low[0, h])
        raw[h] = r
        acc[0] += r * r
        acc[1] += ch[h].astype(F32) * r

    scan(0, kv_state, rest_of_inputs, local_out, finish_out, None)

    sq = jnp.sum(acc[0].T, axis=0, keepdims=True)
    inner = jnp.sum(acc[1].T, axis=0, keepdims=True)
    row = lax.broadcasted_iota(jnp.int32, (8, toks), 0)
    ex_send[...] = jnp.where(row < 4, jnp.broadcast_to(sq, (8, toks)), jnp.broadcast_to(inner, (8, toks)))
    peers = [
        pltpu.make_async_remote_copy(
            src_ref=ex_send, dst_ref=ex_recv.at[d - 1],
            send_sem=ex_s.at[d - 1], recv_sem=ex_r.at[d - 1],
            device_id={"head": (me + d) % nh}, device_id_type=MESH)
        for d in range(1, nh)
    ]
    for peer in peers:
        peer.start()
    total = ex_send[...]
    for d, peer in enumerate(peers):
        peer.wait_recv()
        total = total + ex_recv[d]
    inv = lax.rsqrt(total[0:1] / width + EPSILON)
    slope = inv * (total[4:5] / width)
    acc[0] = jnp.broadcast_to(inv, (dim, toks)).T
    acc[1] = jnp.broadcast_to(inv * slope, (dim, toks)).T

    def qg_state(h):
        g = (acc[0] * (ch[h].astype(F32) - raw[h] * acc[1])).astype(BF16)
        gr[h] = g
        own[1, h] = dot_tn(qh[h], g)

    def local_grads(j):
        for h in (own_base + j, oth_base + j):
            q, k, v, g = qh[h], kh[h], vh[h], gr[h]
            of_head(st0, h)[...] = raw[h] * acc[0]
            first, second = lower(g, v, k)
            of_head(st1, h)[...] = jnp.concatenate([first, second], axis=0) + dot_nt(g, low[0, h])
            first, second = upper(v, g, q)
            raw[h, :CUT] = first
            raw[h, CUT:] = second
            first, second = upper(k, q, g)
            gvp[h, :CUT] = first
            gvp[h, CUT:] = second

    def finish_grads(h):
        of_head(gk_ref, h)[...] = raw[h] + dot_nt(vh[h], low[1, h])
        of_head(gv_ref, h)[...] = gvp[h] + dot(kh[h], low[1, h])

    def early_outs():
        gather(st0, no_ref, heads, 0, toks)
        gather(st1, gq_ref, heads, 0, toks)

    scan(1, qg_state, lambda: None, local_grads, finish_grads, early_outs)

    for peer in peers:
        peer.wait_send()
    for ph in range(2):
        def drain(c, _, ph=ph):
            swap(ph, c).wait_send()
            hand(ph, c).wait_send()

            @pl.when(place(ph) < pairs - 1)
            def _():
                chain(ph, c).wait_send()
            return 0
        lax.fori_loop(0, half, drain, 0)


def write_out(heads, no_ref, gq_ref, gk_ref, gv_ref, no_hbm, gq_hbm, gk_hbm, gv_hbm,
              low_k, low_v, sem, part_sem):
    rows = no_ref.shape[0]
    part = rows // PARTS
    toks = rows // heads
    copies = [
        pltpu.make_async_copy(no_ref, no_hbm, sem.at[0]),
        pltpu.make_async_copy(gq_ref, gq_hbm, sem.at[1]),
    ]
    for copy in copies:
        copy.start()
    for a, (src, low, dst) in enumerate(((gk_ref, low_k, gk_hbm), (gv_ref, low_v, gv_hbm))):
        for j in range(PARTS):
            gather(src, low, heads, j * (toks // PARTS), toks // PARTS)
            at = pl.ds(j * part, part)
            copy = pltpu.make_async_copy(low.at[at], dst.at[at], part_sem.at[a, j])
            copy.start()
            copies.append(copy)
    for copy in copies:
        copy.wait()


def local(n, nh, queries, keys, values, cotangent):
    toks, heads, dim = queries.shape
    rows = toks * heads
    half = heads // 2
    flat = [x.reshape(rows, dim) for x in (queries, keys, values, cotangent)]
    any_spec = pl.BlockSpec(memory_space=pl.ANY)
    sems = pltpu.SemaphoreType.DMA
    per_head = pltpu.VMEM((heads, toks, dim), BF16)
    part = pltpu.VMEM((2, half, dim, dim), F32)
    in_vmem = pl.BlockSpec(memory_space=pltpu.VMEM)
    made = pl.pallas_call(
        functools.partial(kernel, n, nh, heads, toks, dim),
        out_shape=[pltpu.VMEM((rows, dim), BF16)] * 2 + [pltpu.VMEM((rows + heads, dim), F32)] * 2,
        in_specs=[any_spec] * 4,
        out_specs=[in_vmem] * 4,
        scratch_shapes=[
            pltpu.VMEM((2, rows, dim), BF16),
            *[pltpu.VMEM((rows + heads, dim), F32)] * 2,
            *[per_head] * 4,
            *[pltpu.VMEM((heads, toks, dim), F32)] * 2,
            per_head,
            pltpu.VMEM((2, heads, dim, dim), F32),
            *[part] * 5,
            pltpu.VMEM((2, heads, dim, dim), BF16),
            pltpu.VMEM((2, toks, dim), F32),
            pltpu.VMEM((8, toks), F32),
            pltpu.VMEM((nh - 1, 8, toks), F32),
            sems((4,)),
            *[sems((2, half))] * 6,
            sems((nh - 1,)),
            sems((nh - 1,)),
        ],
        compiler_params=pltpu.CompilerParams(
            collective_id=0, has_side_effects=True, vmem_limit_bytes=44 * 2**20),
        cost_estimate=pl.CostEstimate(
            flops=heads * 10 * toks * toks * dim, bytes_accessed=8 * rows * dim, transcendentals=toks),
    )(*flat)
    outs = pl.pallas_call(
        functools.partial(write_out, heads),
        out_shape=[jax.ShapeDtypeStruct((rows, dim), BF16)] * 4,
        in_specs=[in_vmem] * 4,
        out_specs=[any_spec] * 4,
        scratch_shapes=[*[pltpu.VMEM((rows, dim), BF16)] * 2, sems((2,)), sems((2, PARTS))],
        compiler_params=pltpu.CompilerParams(vmem_limit_bytes=16 * 2**20),
        cost_estimate=pl.CostEstimate(flops=0, bytes_accessed=8 * rows * dim, transcendentals=0),
    )(*made)
    return tuple(x.reshape(toks, heads, dim) for x in outs)


def solution(mesh):
    n, nh = mesh.shape["seq"], mesh.shape["head"]
    spec = P("seq", "head", None)
    return jax.shard_map(
        functools.partial(local, n, nh),
        mesh=mesh,
        in_specs=(spec,) * 4,
        out_specs=(spec,) * 4,
        check_vma=False,
    )
```

```python
import functools

import jax
import jax.numpy as jnp
from jax import lax
from jax.experimental import pallas as pl
from jax.experimental.pallas import tpu as pltpu
from jax.sharding import PartitionSpec as P

EPSILON = 1e-06
CUT = 256
PARTS = 4
PIECES = 2
TOKS_STEP = 16
F32 = jnp.float32
BF16 = jnp.bfloat16
MESH = pl.DeviceIdType.MESH


def dot(a, b):
    return lax.dot_general(a, b, (((1,), (0,)), ((), ())), preferred_element_type=F32)


def dot_nt(a, b):
    return lax.dot_general(a, b, (((1,), (1,)), ((), ())), preferred_element_type=F32)


def dot_tn(a, b):
    return lax.dot_general(a, b, (((0,), (0,)), ((), ())), preferred_element_type=F32)


def token_rows(heads, token, group):
    return pl.ds(group * 8 * (token[1] + 1) + token[0], 8, stride=token[1] + 1)


def spread(src, dst, heads, groups):
    toks = src.shape[0] // heads

    def body(j, _):
        start = j * TOKS_STEP
        x = src[pl.ds(pl.multiple_of(start * heads, TOKS_STEP * heads), TOKS_STEP * heads), :].astype(F32)
        for t in range(TOKS_STEP):
            for group in groups:
                at = t * heads + group * 8
                dst[token_rows(heads, (start + t, toks), group), :] = x[at:at + 8]
        return 0
    lax.fori_loop(0, toks // TOKS_STEP, body, 0)


def gather(src, dst, heads, first, count):
    toks = dst.shape[0] // heads

    def body(j, _):
        start = first + j * TOKS_STEP
        x = jnp.concatenate([
            src[token_rows(heads, (start + t, toks), group), :]
            for t in range(TOKS_STEP) for group in range(heads // 8)
        ], axis=0)
        at = pl.ds(pl.multiple_of(start * heads, TOKS_STEP * heads), TOKS_STEP * heads)
        dst[at, :] = x.astype(BF16)
        return 0
    lax.fori_loop(0, count // TOKS_STEP, body, 0)


def kernel(n, nh, heads, toks, dim,
           q_hbm, k_hbm, v_hbm, c_hbm, no_ref, gq_ref, gk_ref, gv_ref,
           io, st0, st1, qh, kh, vh, ch, raw, gvp, gr,
           own, rs, rp, rx, sp, sx, low, acc, ex_send, ex_recv,
           in_sem, rs_s, rs_r, rp_s, rp_r, rx_s, rx_r, ex_s, ex_r):
    half = heads // 2
    pairs = n // 2
    rows = toks * heads
    width = heads * nh * dim
    seq = lax.axis_index("seq")
    me = lax.axis_index("head")
    pair = seq // 2
    side = seq % 2
    partner = seq + 1 - 2 * side
    own_base = side * half
    oth_base = (1 - side) * half

    landing = (no_ref, gq_ref, io.at[0], io.at[1])
    stages = (st0, st1, gk_ref, gv_ref)
    loads = [
        pltpu.make_async_copy(src, landing[a], in_sem.at[a])
        for a, src in enumerate((k_hbm, v_hbm, q_hbm, c_hbm))
    ]
    loads[0].start()
    loads[1].start()

    barrier = pltpu.get_barrier_semaphore()
    pl.semaphore_signal(barrier, inc=1, device_id={"seq": partner}, device_id_type=MESH)

    @pl.when(pair > 0)
    def _():
        pl.semaphore_signal(barrier, inc=1, device_id={"seq": (seq + n - 2) % n}, device_id_type=MESH)

    @pl.when(pair < pairs - 1)
    def _():
        pl.semaphore_signal(barrier, inc=1, device_id={"seq": (seq + 2) % n}, device_id_type=MESH)

    for d in range(1, nh):
        pl.semaphore_signal(barrier, inc=1, device_id={"head": (me + d) % nh}, device_id_type=MESH)

    def of_head(ref, h):
        return ref.at[pl.ds(h * (toks + 1), toks), :]

    def swap(ph, c):
        return pltpu.make_async_remote_copy(
            src_ref=own.at[ph, oth_base + c], dst_ref=rs.at[ph, c],
            send_sem=rs_s.at[ph, c], recv_sem=rs_r.at[ph, c],
            device_id={"seq": partner}, device_id_type=MESH)

    def chain(ph, c, piece):
        nxt = (seq + 2) % n if ph == 0 else (seq + n - 2) % n
        return pltpu.make_async_remote_copy(
            src_ref=sp.at[ph, c, rows_of(piece)], dst_ref=rp.at[ph, c, rows_of(piece)],
            send_sem=rp_s.at[ph, c, piece], recv_sem=rp_r.at[ph, c, piece],
            device_id={"seq": nxt}, device_id_type=MESH)

    def hand(ph, c):
        return pltpu.make_async_remote_copy(
            src_ref=sx.at[ph, c], dst_ref=rx.at[ph, c],
            send_sem=rx_s.at[ph, c], recv_sem=rx_r.at[ph, c],
            device_id={"seq": partner}, device_id_type=MESH)

    def place(ph):
        return pair if ph == 0 else pairs - 1 - pair

    def rows_of(piece):
        return pl.ds(piece * (dim // PIECES), dim // PIECES)

    def relay(ph, c):
        at = place(ph)
        later = (side == 1) if ph == 0 else (side == 0)
        swap(ph, c).wait_recv()
        for piece in range(PIECES):
            some = rows_of(piece)
            mine = own[ph, own_base + c, some, :]
            theirs = rs[ph, c, some, :]

            @pl.when(at > 0)
            def _():
                chain(ph, c, piece).wait_recv()

            so_far = rp[ph, c, some, :]

            @pl.when(at < pairs - 1)
            def _():
                sp[ph, c, some, :] = so_far + (mine + theirs)
                chain(ph, c, piece).start()

            sx[ph, c, some, :] = so_far + jnp.where(later, 0.0, mine)
            low[ph, own_base + c, some, :] = (so_far + jnp.where(later, theirs, 0.0)).astype(BF16)

    def take(ph, c):
        hand(ph, c).wait_recv()
        low[ph, oth_base + c] = rx[ph, c].astype(BF16)

    def scan(ph, state, ahead, before, unit, finish, after):
        at = place(ph)

        def units_by(c):
            lead = half * at // (2 * (pairs - 1)) + (c + 1) * at // (pairs - 1)
            return jnp.where(c < 0, 0, jnp.minimum(half, lead))

        def others_by(c):
            return jnp.where(at == 0, jnp.clip(c + 4, 0, half), half)

        def owns_by(c):
            return jnp.where(c < 0, 0, jnp.maximum(c + 1, units_by(c)))

        def finished_by(c):
            return jnp.where(c < 0, 0, jnp.minimum(c + 1, units_by(c)))

        defer = half * (pairs - 1 - at) // (pairs - 1)

        def hands_by(c):
            return jnp.clip(c + 1 - defer, 0, half)

        def takes_by(c):
            return jnp.clip(c - 1 - defer, 0, units_by(c))

        def run(low_end, high_end, step):
            def body(c, _):
                step(c)
                return 0
            lax.fori_loop(low_end, high_end, body, 0)

        def other(c):
            state(oth_base + c)
            swap(ph, c).start()

        def give(c):
            hand(ph, c).start()

        def take_one(c):
            take(ph, c)
            finish(oth_base + c)

        def slot(c):
            run(others_by(c - 1), others_by(c), other)
            run(owns_by(c - 1), owns_by(c), lambda j: state(own_base + j))
            run(units_by(c - 1), units_by(c), unit)
            if after is not None:
                @pl.when((units_by(c) == half) & (units_by(c - 1) < half))
                def _():
                    after()
            relay(ph, c)
            run(hands_by(c - 1), hands_by(c), give)
            run(finished_by(c - 1), finished_by(c), lambda j: finish(own_base + j))
            run(takes_by(c - 1), takes_by(c), take_one)

        run(0, others_by(-1), other)
        if ahead is not None:
            ahead()
        if before is not None:
            pl.when(at > 0)(before)
        run(0, half, slot)
        run(hands_by(half - 1), half, give)
        if before is not None:
            pl.when(at == 0)(before)
        run(units_by(half - 1), half, unit)
        if after is not None:
            @pl.when(units_by(half - 1) < half)
            def _():
                after()
        run(finished_by(half - 1), half, lambda j: finish(own_base + j))
        run(takes_by(half - 1), half, take_one)

    for ph in range(2):
        @pl.when(place(ph) == 0)
        def _():
            rp[ph] = jnp.zeros(rp.shape[1:], F32)

    acc[...] = jnp.zeros(acc.shape, F32)
    loads[0].wait()
    loads[2].start()
    loads[3].start()
    all_groups = range(heads // 8)
    by_half = half % 8 == 0

    def spread_half(a, which):
        def of(groups):
            spread(landing[a], stages[a], heads, groups)

        if by_half:
            pl.when(which == 0)(lambda: of(range(half // 8)))
            pl.when(which == 1)(lambda: of(range(half // 8, heads // 8)))
        else:
            of(all_groups)

    spread_half(0, 1 - side)
    loads[1].wait()
    spread_half(1, 1 - side)
    pl.semaphore_wait(
        barrier, nh + jnp.where(pair > 0, 1, 0) + jnp.where(pair < pairs - 1, 1, 0))

    def kv_state(h):
        k = of_head(st0, h)[...].astype(BF16)
        v = of_head(st1, h)[...].astype(BF16)
        kh[h] = k
        vh[h] = v
        own[0, h] = dot_tn(k, v)

    def rest_of_keys():
        if by_half:
            spread_half(0, side)
            spread_half(1, side)

    def rest_of_inputs():
        loads[2].wait()
        spread(landing[2], stages[2], heads, all_groups)
        loads[3].wait()
        spread(landing[3], stages[3], heads, all_groups)

    def square(compare):
        return compare(lax.broadcasted_iota(jnp.int32, (CUT, CUT), 1),
                       lax.broadcasted_iota(jnp.int32, (CUT, CUT), 0))

    def keep(mask, x):
        return jnp.where(mask, x, 0.0).astype(BF16)

    def lower(a, b, c):
        mask = square(jnp.less_equal)
        w0 = keep(mask, dot_nt(a[:CUT], b[:CUT]))
        w1 = dot_nt(a[CUT:], b)
        w1 = jnp.concatenate([w1[:, :CUT].astype(BF16), keep(mask, w1[:, CUT:])], axis=1)
        return dot(w0, c[:CUT]), dot(w1, c)

    def upper(a, b, c):
        mask = square(jnp.greater_equal)
        w0 = dot_nt(a[:CUT], b)
        w0 = jnp.concatenate([keep(mask, w0[:, :CUT]), w0[:, CUT:].astype(BF16)], axis=1)
        w1 = keep(mask, dot_nt(a[CUT:], b[CUT:]))
        return dot(w0, c), dot(w1, c[CUT:])

    def local_out(j):
        for h in (own_base + j, oth_base + j):
            q = of_head(gk_ref, h)[...].astype(BF16)
            qh[h] = q
            ch[h] = of_head(gv_ref, h)[...].astype(BF16)
            first, second = lower(q, kh[h], vh[h])
            raw[h, :CUT] = first
            raw[h, CUT:] = second

    def finish_out(h):
        r = raw[h] + dot(qh[h], low[0, h])
        raw[h] = r
        acc[0] += r * r
        acc[1] += ch[h].astype(F32) * r

    scan(0, kv_state, rest_of_keys, rest_of_inputs, local_out, finish_out, None)

    sq = jnp.sum(acc[0].T, axis=0, keepdims=True)
    inner = jnp.sum(acc[1].T, axis=0, keepdims=True)
    row = lax.broadcasted_iota(jnp.int32, (8, toks), 0)
    ex_send[...] = jnp.where(row < 4, jnp.broadcast_to(sq, (8, toks)), jnp.broadcast_to(inner, (8, toks)))
    peers = [
        pltpu.make_async_remote_copy(
            src_ref=ex_send, dst_ref=ex_recv.at[d - 1],
            send_sem=ex_s.at[d - 1], recv_sem=ex_r.at[d - 1],
            device_id={"head": (me + d) % nh}, device_id_type=MESH)
        for d in range(1, nh)
    ]
    for peer in peers:
        peer.start()
    total = ex_send[...]
    for d, peer in enumerate(peers):
        peer.wait_recv()
        total = total + ex_recv[d]
    inv = lax.rsqrt(total[0:1] / width + EPSILON)
    slope = inv * (total[4:5] / width)
    acc[0] = jnp.broadcast_to(inv, (dim, toks)).T
    acc[1] = jnp.broadcast_to(inv * slope, (dim, toks)).T

    def qg_state(h):
        g = (acc[0] * (ch[h].astype(F32) - raw[h] * acc[1])).astype(BF16)
        gr[h] = g
        own[1, h] = dot_tn(qh[h], g)

    def local_grads(j):
        for h in (own_base + j, oth_base + j):
            q, k, v, g = qh[h], kh[h], vh[h], gr[h]
            of_head(st0, h)[...] = raw[h] * acc[0]
            first, second = lower(g, v, k)
            of_head(st1, h)[...] = jnp.concatenate([first, second], axis=0) + dot_nt(g, low[0, h])
            first, second = upper(v, g, q)
            raw[h, :CUT] = first
            raw[h, CUT:] = second
            first, second = upper(k, q, g)
            gvp[h, :CUT] = first
            gvp[h, CUT:] = second

    def finish_grads(h):
        of_head(gk_ref, h)[...] = raw[h] + dot_nt(vh[h], low[1, h])
        of_head(gv_ref, h)[...] = gvp[h] + dot(kh[h], low[1, h])

    def early_outs():
        gather(st0, no_ref, heads, 0, toks)
        gather(st1, gq_ref, heads, 0, toks)

    scan(1, qg_state, None, None, local_grads, finish_grads, early_outs)

    for peer in peers:
        peer.wait_send()
    for ph in range(2):
        def drain(c, _, ph=ph):
            swap(ph, c).wait_send()
            hand(ph, c).wait_send()

            @pl.when(place(ph) < pairs - 1)
            def _():
                for piece in range(PIECES):
                    chain(ph, c, piece).wait_send()
            return 0
        lax.fori_loop(0, half, drain, 0)


def write_out(heads, no_ref, gq_ref, gk_ref, gv_ref, no_hbm, gq_hbm, gk_hbm, gv_hbm,
              low_k, low_v, sem, part_sem):
    rows = no_ref.shape[0]
    part = rows // PARTS
    toks = rows // heads
    copies = [
        pltpu.make_async_copy(no_ref, no_hbm, sem.at[0]),
        pltpu.make_async_copy(gq_ref, gq_hbm, sem.at[1]),
    ]
    for copy in copies:
        copy.start()
    for a, (src, low, dst) in enumerate(((gk_ref, low_k, gk_hbm), (gv_ref, low_v, gv_hbm))):
        for j in range(PARTS):
            gather(src, low, heads, j * (toks // PARTS), toks // PARTS)
            at = pl.ds(j * part, part)
            copy = pltpu.make_async_copy(low.at[at], dst.at[at], part_sem.at[a, j])
            copy.start()
            copies.append(copy)
    for copy in copies:
        copy.wait()


def local(n, nh, queries, keys, values, cotangent):
    toks, heads, dim = queries.shape
    rows = toks * heads
    half = heads // 2
    flat = [x.reshape(rows, dim) for x in (queries, keys, values, cotangent)]
    any_spec = pl.BlockSpec(memory_space=pl.ANY)
    sems = pltpu.SemaphoreType.DMA
    per_head = pltpu.VMEM((heads, toks, dim), BF16)
    part = pltpu.VMEM((2, half, dim, dim), F32)
    in_vmem = pl.BlockSpec(memory_space=pltpu.VMEM)
    made = pl.pallas_call(
        functools.partial(kernel, n, nh, heads, toks, dim),
        out_shape=[pltpu.VMEM((rows, dim), BF16)] * 2 + [pltpu.VMEM((rows + heads, dim), F32)] * 2,
        in_specs=[any_spec] * 4,
        out_specs=[in_vmem] * 4,
        scratch_shapes=[
            pltpu.VMEM((2, rows, dim), BF16),
            *[pltpu.VMEM((rows + heads, dim), F32)] * 2,
            *[per_head] * 4,
            *[pltpu.VMEM((heads, toks, dim), F32)] * 2,
            per_head,
            pltpu.VMEM((2, heads, dim, dim), F32),
            *[part] * 5,
            pltpu.VMEM((2, heads, dim, dim), BF16),
            pltpu.VMEM((2, toks, dim), F32),
            pltpu.VMEM((8, toks), F32),
            pltpu.VMEM((nh - 1, 8, toks), F32),
            sems((4,)),
            *[sems((2, half))] * 2,
            *[sems((2, half, PIECES))] * 2,
            *[sems((2, half))] * 2,
            sems((nh - 1,)),
            sems((nh - 1,)),
        ],
        compiler_params=pltpu.CompilerParams(
            collective_id=0, has_side_effects=True, vmem_limit_bytes=44 * 2**20),
        cost_estimate=pl.CostEstimate(
            flops=heads * 10 * toks * toks * dim, bytes_accessed=8 * rows * dim, transcendentals=toks),
    )(*flat)
    outs = pl.pallas_call(
        functools.partial(write_out, heads),
        out_shape=[jax.ShapeDtypeStruct((rows, dim), BF16)] * 4,
        in_specs=[in_vmem] * 4,
        out_specs=[any_spec] * 4,
        scratch_shapes=[*[pltpu.VMEM((rows, dim), BF16)] * 2, sems((2,)), sems((2, PARTS))],
        compiler_params=pltpu.CompilerParams(vmem_limit_bytes=16 * 2**20),
        cost_estimate=pl.CostEstimate(flops=0, bytes_accessed=8 * rows * dim, transcendentals=0),
    )(*made)
    return tuple(x.reshape(toks, heads, dim) for x in outs)


def solution(mesh):
    n, nh = mesh.shape["seq"], mesh.shape["head"]
    spec = P("seq", "head", None)
    return jax.shard_map(
        functools.partial(local, n, nh),
        mesh=mesh,
        in_specs=(spec,) * 4,
        out_specs=(spec,) * 4,
        check_vma=False,
    )
```

```python
import functools

import jax
import jax.numpy as jnp
from jax import lax
from jax.experimental import pallas as pl
from jax.experimental.pallas import tpu as pltpu
from jax.sharding import PartitionSpec as P

EPSILON = 1e-06
CUT = 256
PARTS = 4
PIECES = 2
TOKS_STEP = 16
F32 = jnp.float32
BF16 = jnp.bfloat16
MESH = pl.DeviceIdType.MESH


def dot(a, b):
    return lax.dot_general(a, b, (((1,), (0,)), ((), ())), preferred_element_type=F32)


def dot_nt(a, b):
    return lax.dot_general(a, b, (((1,), (1,)), ((), ())), preferred_element_type=F32)


def dot_tn(a, b):
    return lax.dot_general(a, b, (((0,), (0,)), ((), ())), preferred_element_type=F32)


def token_rows(heads, token, group):
    return pl.ds(group * 8 * (token[1] + 1) + token[0], 8, stride=token[1] + 1)


def spread(src, dst, heads, groups):
    toks = src.shape[0] // heads

    def body(j, _):
        start = j * TOKS_STEP
        x = src[pl.ds(pl.multiple_of(start * heads, TOKS_STEP * heads), TOKS_STEP * heads), :].astype(F32)
        for t in range(TOKS_STEP):
            for group in groups:
                at = t * heads + group * 8
                dst[token_rows(heads, (start + t, toks), group), :] = x[at:at + 8]
        return 0
    lax.fori_loop(0, toks // TOKS_STEP, body, 0)


def gather(src, dst, heads, first, count):
    toks = dst.shape[0] // heads

    def body(j, _):
        start = first + j * TOKS_STEP
        x = jnp.concatenate([
            src[token_rows(heads, (start + t, toks), group), :]
            for t in range(TOKS_STEP) for group in range(heads // 8)
        ], axis=0)
        at = pl.ds(pl.multiple_of(start * heads, TOKS_STEP * heads), TOKS_STEP * heads)
        dst[at, :] = x.astype(BF16)
        return 0
    lax.fori_loop(0, count // TOKS_STEP, body, 0)


def kernel(n, nh, heads, toks, dim,
           q_hbm, k_hbm, v_hbm, c_hbm, no_ref, gq_ref, gk_ref, gv_ref,
           io, st0, st1, qh, kh, vh, ch, raw, gvp, gr,
           own, rs, rp, rx, sp, sx, low, acc, ex_send, ex_recv,
           in_sem, rs_s, rs_r, rp_s, rp_r, rx_s, rx_r, ex_s, ex_r):
    half = heads // 2
    pairs = n // 2
    rows = toks * heads
    width = heads * nh * dim
    seq = lax.axis_index("seq")
    me = lax.axis_index("head")
    pair = seq // 2
    side = seq % 2
    partner = seq + 1 - 2 * side
    own_base = side * half
    oth_base = (1 - side) * half

    landing = (no_ref, gq_ref, io.at[0], io.at[1])
    stages = (st0, st1, gk_ref, gv_ref)
    loads = [
        pltpu.make_async_copy(src, landing[a], in_sem.at[a])
        for a, src in enumerate((k_hbm, v_hbm, q_hbm, c_hbm))
    ]
    loads[0].start()
    loads[1].start()

    barrier = pltpu.get_barrier_semaphore()
    pl.semaphore_signal(barrier, inc=1, device_id={"seq": partner}, device_id_type=MESH)

    @pl.when(pair > 0)
    def _():
        pl.semaphore_signal(barrier, inc=1, device_id={"seq": (seq + n - 2) % n}, device_id_type=MESH)

    @pl.when(pair < pairs - 1)
    def _():
        pl.semaphore_signal(barrier, inc=1, device_id={"seq": (seq + 2) % n}, device_id_type=MESH)

    for d in range(1, nh):
        pl.semaphore_signal(barrier, inc=1, device_id={"head": (me + d) % nh}, device_id_type=MESH)

    def of_head(ref, h):
        return ref.at[pl.ds(h * (toks + 1), toks), :]

    def swap(ph, c):
        return pltpu.make_async_remote_copy(
            src_ref=own.at[ph, oth_base + c], dst_ref=rs.at[ph, c],
            send_sem=rs_s.at[ph, c], recv_sem=rs_r.at[ph, c],
            device_id={"seq": partner}, device_id_type=MESH)

    def chain(ph, c, piece):
        nxt = (seq + 2) % n if ph == 0 else (seq + n - 2) % n
        return pltpu.make_async_remote_copy(
            src_ref=sp.at[ph, c, rows_of(piece)], dst_ref=rp.at[ph, c, rows_of(piece)],
            send_sem=rp_s.at[ph, c, piece], recv_sem=rp_r.at[ph, c, piece],
            device_id={"seq": nxt}, device_id_type=MESH)

    def hand(ph, c):
        return pltpu.make_async_remote_copy(
            src_ref=sx.at[ph, c], dst_ref=rx.at[ph, c],
            send_sem=rx_s.at[ph, c], recv_sem=rx_r.at[ph, c],
            device_id={"seq": partner}, device_id_type=MESH)

    def place(ph):
        return pair if ph == 0 else pairs - 1 - pair

    def rows_of(piece):
        return pl.ds(piece * (dim // PIECES), dim // PIECES)

    def relay(ph, c):
        at = place(ph)
        later = (side == 1) if ph == 0 else (side == 0)
        swap(ph, c).wait_recv()
        for piece in range(PIECES):
            some = rows_of(piece)
            mine = own[ph, own_base + c, some, :]
            theirs = rs[ph, c, some, :]

            @pl.when(at > 0)
            def _():
                chain(ph, c, piece).wait_recv()

            so_far = rp[ph, c, some, :]

            @pl.when(at < pairs - 1)
            def _():
                sp[ph, c, some, :] = so_far + (mine + theirs)
                chain(ph, c, piece).start()

            sx[ph, c, some, :] = so_far + jnp.where(later, 0.0, mine)
            low[ph, own_base + c, some, :] = (so_far + jnp.where(later, theirs, 0.0)).astype(BF16)

    def take(ph, c):
        hand(ph, c).wait_recv()
        low[ph, oth_base + c] = rx[ph, c].astype(BF16)

    batch = 4 if half % 4 == 0 else 1

    def scan(ph, state, ahead, before, unit, finish, after):
        at = place(ph)

        def units_by(c):
            lead = half * at // (2 * (pairs - 1)) + (c + 1) * at // (pairs - 1)
            return jnp.where(c < 0, 0, jnp.minimum(half, lead))

        defer = half * (pairs - 1 - at) // (pairs - 1)

        def hands_by(c):
            return jnp.clip(c + 1 - defer, 0, half)

        def takes_by(c):
            return jnp.clip(c - 1 - defer, 0, units_by(c))

        def run(low_end, high_end, step):
            def body(c, _):
                step(c)
                return 0
            lax.fori_loop(low_end, high_end, body, 0)

        def give(c):
            hand(ph, c).start()

        def others(j):
            state([oth_base + j * batch + i for i in range(batch)])
            for i in range(batch):
                swap(ph, j * batch + i).start()

        def owns(j):
            state([own_base + j * batch + i for i in range(batch)])

        def take_one(c):
            take(ph, c)
            finish([own_base + c, oth_base + c])

        def slot(c):
            run(units_by(c - 1), units_by(c), unit)
            if after is not None:
                @pl.when((units_by(c) == half) & (units_by(c - 1) < half))
                def _():
                    after()
            relay(ph, c)
            run(hands_by(c - 1), hands_by(c), give)
            run(takes_by(c - 1), takes_by(c), take_one)

        run(0, half // batch, others)
        if ahead is not None:
            ahead()
        run(0, half // batch, owns)
        if before is not None:
            pl.when(at > 0)(before)
        run(0, half, slot)
        run(hands_by(half - 1), half, give)
        if before is not None:
            pl.when(at == 0)(before)
        run(units_by(half - 1), half, unit)
        if after is not None:
            @pl.when(units_by(half - 1) < half)
            def _():
                after()
        run(takes_by(half - 1), half, take_one)

    for ph in range(2):
        @pl.when(place(ph) == 0)
        def _():
            rp[ph] = jnp.zeros(rp.shape[1:], F32)

    acc[...] = jnp.zeros(acc.shape, F32)
    loads[0].wait()
    loads[2].start()
    loads[3].start()
    all_groups = range(heads // 8)
    by_half = half % 8 == 0

    def spread_half(a, which):
        def of(groups):
            spread(landing[a], stages[a], heads, groups)

        if by_half:
            pl.when(which == 0)(lambda: of(range(half // 8)))
            pl.when(which == 1)(lambda: of(range(half // 8, heads // 8)))
        else:
            of(all_groups)

    spread_half(0, 1 - side)
    loads[1].wait()
    spread_half(1, 1 - side)
    pl.semaphore_wait(
        barrier, nh + jnp.where(pair > 0, 1, 0) + jnp.where(pair < pairs - 1, 1, 0))

    def kv_state(at_once):
        for h in at_once:
            k = of_head(st0, h)[...].astype(BF16)
            v = of_head(st1, h)[...].astype(BF16)
            kh[h] = k
            vh[h] = v
            own[0, h] = dot_tn(k, v)

    def rest_of_keys():
        if by_half:
            spread_half(0, side)
            spread_half(1, side)

    def rest_of_inputs():
        loads[2].wait()
        spread(landing[2], stages[2], heads, all_groups)
        loads[3].wait()
        spread(landing[3], stages[3], heads, all_groups)

    def square(compare):
        return compare(lax.broadcasted_iota(jnp.int32, (CUT, CUT), 1),
                       lax.broadcasted_iota(jnp.int32, (CUT, CUT), 0))

    def keep(mask, x):
        return jnp.where(mask, x, 0.0).astype(BF16)

    def lower(a, b, c):
        mask = square(jnp.less_equal)
        w0 = keep(mask, dot_nt(a[:CUT], b[:CUT]))
        w1 = dot_nt(a[CUT:], b)
        w1 = jnp.concatenate([w1[:, :CUT].astype(BF16), keep(mask, w1[:, CUT:])], axis=1)
        return dot(w0, c[:CUT]), dot(w1, c)

    def upper(a, b, c):
        mask = square(jnp.greater_equal)
        w0 = dot_nt(a[:CUT], b)
        w0 = jnp.concatenate([keep(mask, w0[:, :CUT]), w0[:, CUT:].astype(BF16)], axis=1)
        w1 = keep(mask, dot_nt(a[CUT:], b[CUT:]))
        return dot(w0, c), dot(w1, c[CUT:])

    def local_out(j):
        for h in (own_base + j, oth_base + j):
            q = of_head(gk_ref, h)[...].astype(BF16)
            qh[h] = q
            ch[h] = of_head(gv_ref, h)[...].astype(BF16)
            first, second = lower(q, kh[h], vh[h])
            raw[h, :CUT] = first
            raw[h, CUT:] = second

    blocks = [pl.ds(start, CUT // 2) for start in range(0, toks, CUT // 2)]

    def finish_out(at_once):
        for some in blocks:
            squares, products = acc[0, some, :], acc[1, some, :]
            for h in at_once:
                r = raw[h, some, :] + dot(qh[h, some, :], low[0, h])
                raw[h, some, :] = r
                squares += r * r
                products += ch[h, some, :].astype(F32) * r
            acc[0, some, :] = squares
            acc[1, some, :] = products

    scan(0, kv_state, rest_of_keys, rest_of_inputs, local_out, finish_out, None)

    sq = jnp.sum(acc[0].T, axis=0, keepdims=True)
    inner = jnp.sum(acc[1].T, axis=0, keepdims=True)
    row = lax.broadcasted_iota(jnp.int32, (8, toks), 0)
    ex_send[...] = jnp.where(row < 4, jnp.broadcast_to(sq, (8, toks)), jnp.broadcast_to(inner, (8, toks)))
    peers = [
        pltpu.make_async_remote_copy(
            src_ref=ex_send, dst_ref=ex_recv.at[d - 1],
            send_sem=ex_s.at[d - 1], recv_sem=ex_r.at[d - 1],
            device_id={"head": (me + d) % nh}, device_id_type=MESH)
        for d in range(1, nh)
    ]
    for peer in peers:
        peer.start()
    total = ex_send[...]
    for d, peer in enumerate(peers):
        peer.wait_recv()
        total = total + ex_recv[d]
    inv = lax.rsqrt(total[0:1] / width + EPSILON)
    slope = inv * (total[4:5] / width)
    acc[0] = jnp.broadcast_to(inv, (dim, toks)).T
    acc[1] = jnp.broadcast_to(inv * slope, (dim, toks)).T

    def qg_state(at_once):
        for h in at_once:
            for some in blocks:
                gr[h, some, :] = (acc[0, some, :] * (
                    ch[h, some, :].astype(F32) - raw[h, some, :] * acc[1, some, :])).astype(BF16)
            own[1, h] = dot_tn(qh[h], gr[h])

    def local_grads(j):
        for h in (own_base + j, oth_base + j):
            q, k, v, g = qh[h], kh[h], vh[h], gr[h]
            of_head(st0, h)[...] = raw[h] * acc[0]
            first, second = lower(g, v, k)
            of_head(st1, h)[...] = jnp.concatenate([first, second], axis=0) + dot_nt(g, low[0, h])
            first, second = upper(v, g, q)
            raw[h, :CUT] = first
            raw[h, CUT:] = second
            first, second = upper(k, q, g)
            gvp[h, :CUT] = first
            gvp[h, CUT:] = second

    def finish_grads(at_once):
        for h in at_once:
            of_head(gk_ref, h)[...] = raw[h] + dot_nt(vh[h], low[1, h])
            of_head(gv_ref, h)[...] = gvp[h] + dot(kh[h], low[1, h])

    def early_outs():
        gather(st0, no_ref, heads, 0, toks)
        gather(st1, gq_ref, heads, 0, toks)

    scan(1, qg_state, None, None, local_grads, finish_grads, early_outs)

    for peer in peers:
        peer.wait_send()
    for ph in range(2):
        def drain(c, _, ph=ph):
            swap(ph, c).wait_send()
            hand(ph, c).wait_send()

            @pl.when(place(ph) < pairs - 1)
            def _():
                for piece in range(PIECES):
                    chain(ph, c, piece).wait_send()
            return 0
        lax.fori_loop(0, half, drain, 0)


def write_out(heads, no_ref, gq_ref, gk_ref, gv_ref, no_hbm, gq_hbm, gk_hbm, gv_hbm,
              low_k, low_v, sem, part_sem):
    rows = no_ref.shape[0]
    part = rows // PARTS
    toks = rows // heads
    copies = [
        pltpu.make_async_copy(no_ref, no_hbm, sem.at[0]),
        pltpu.make_async_copy(gq_ref, gq_hbm, sem.at[1]),
    ]
    for copy in copies:
        copy.start()
    for a, (src, low, dst) in enumerate(((gk_ref, low_k, gk_hbm), (gv_ref, low_v, gv_hbm))):
        for j in range(PARTS):
            gather(src, low, heads, j * (toks // PARTS), toks // PARTS)
            at = pl.ds(j * part, part)
            copy = pltpu.make_async_copy(low.at[at], dst.at[at], part_sem.at[a, j])
            copy.start()
            copies.append(copy)
    for copy in copies:
        copy.wait()


def local(n, nh, queries, keys, values, cotangent):
    toks, heads, dim = queries.shape
    rows = toks * heads
    half = heads // 2
    flat = [x.reshape(rows, dim) for x in (queries, keys, values, cotangent)]
    any_spec = pl.BlockSpec(memory_space=pl.ANY)
    sems = pltpu.SemaphoreType.DMA
    per_head = pltpu.VMEM((heads, toks, dim), BF16)
    part = pltpu.VMEM((2, half, dim, dim), F32)
    in_vmem = pl.BlockSpec(memory_space=pltpu.VMEM)
    made = pl.pallas_call(
        functools.partial(kernel, n, nh, heads, toks, dim),
        out_shape=[pltpu.VMEM((rows, dim), BF16)] * 2 + [pltpu.VMEM((rows + heads, dim), F32)] * 2,
        in_specs=[any_spec] * 4,
        out_specs=[in_vmem] * 4,
        scratch_shapes=[
            pltpu.VMEM((2, rows, dim), BF16),
            *[pltpu.VMEM((rows + heads, dim), F32)] * 2,
            *[per_head] * 4,
            *[pltpu.VMEM((heads, toks, dim), F32)] * 2,
            per_head,
            pltpu.VMEM((2, heads, dim, dim), F32),
            *[part] * 5,
            pltpu.VMEM((2, heads, dim, dim), BF16),
            pltpu.VMEM((2, toks, dim), F32),
            pltpu.VMEM((8, toks), F32),
            pltpu.VMEM((nh - 1, 8, toks), F32),
            sems((4,)),
            *[sems((2, half))] * 2,
            *[sems((2, half, PIECES))] * 2,
            *[sems((2, half))] * 2,
            sems((nh - 1,)),
            sems((nh - 1,)),
        ],
        compiler_params=pltpu.CompilerParams(
            collective_id=0, has_side_effects=True, vmem_limit_bytes=44 * 2**20),
        cost_estimate=pl.CostEstimate(
            flops=heads * 10 * toks * toks * dim, bytes_accessed=8 * rows * dim, transcendentals=toks),
    )(*flat)
    outs = pl.pallas_call(
        functools.partial(write_out, heads),
        out_shape=[jax.ShapeDtypeStruct((rows, dim), BF16)] * 4,
        in_specs=[in_vmem] * 4,
        out_specs=[any_spec] * 4,
        scratch_shapes=[*[pltpu.VMEM((rows, dim), BF16)] * 2, sems((2,)), sems((2, PARTS))],
        compiler_params=pltpu.CompilerParams(vmem_limit_bytes=16 * 2**20),
        cost_estimate=pl.CostEstimate(flops=0, bytes_accessed=8 * rows * dim, transcendentals=0),
    )(*made)
    return tuple(x.reshape(toks, heads, dim) for x in outs)


def solution(mesh):
    n, nh = mesh.shape["seq"], mesh.shape["head"]
    spec = P("seq", "head", None)
    return jax.shard_map(
        functools.partial(local, n, nh),
        mesh=mesh,
        in_specs=(spec,) * 4,
        out_specs=(spec,) * 4,
        check_vma=False,
    )
```

```python
import functools

import jax
import jax.numpy as jnp
from jax import lax
from jax.experimental import pallas as pl
from jax.experimental.pallas import tpu as pltpu
from jax.sharding import PartitionSpec as P

EPSILON = 1e-06
CUT = 256
PARTS = 4
PIECES = 2
TOKS_STEP = 16
F32 = jnp.float32
BF16 = jnp.bfloat16
MESH = pl.DeviceIdType.MESH


def dot(a, b):
    return lax.dot_general(a, b, (((1,), (0,)), ((), ())), preferred_element_type=F32)


def dot_nt(a, b):
    return lax.dot_general(a, b, (((1,), (1,)), ((), ())), preferred_element_type=F32)


def dot_tn(a, b):
    return lax.dot_general(a, b, (((0,), (0,)), ((), ())), preferred_element_type=F32)


def token_rows(heads, token, group):
    return pl.ds(group * 8 * (token[1] + 1) + token[0], 8, stride=token[1] + 1)


def spread(src, dst, heads, groups):
    toks = src.shape[0] // heads

    def body(j, _):
        start = j * TOKS_STEP
        x = src[pl.ds(pl.multiple_of(start * heads, TOKS_STEP * heads), TOKS_STEP * heads), :].astype(F32)
        for t in range(TOKS_STEP):
            for group in groups:
                at = t * heads + group * 8
                dst[token_rows(heads, (start + t, toks), group), :] = x[at:at + 8]
        return 0
    lax.fori_loop(0, toks // TOKS_STEP, body, 0)


def gather(src, dst, heads, first, count):
    toks = dst.shape[0] // heads

    def body(j, _):
        start = first + j * TOKS_STEP
        x = jnp.concatenate([
            src[token_rows(heads, (start + t, toks), group), :]
            for t in range(TOKS_STEP) for group in range(heads // 8)
        ], axis=0)
        at = pl.ds(pl.multiple_of(start * heads, TOKS_STEP * heads), TOKS_STEP * heads)
        dst[at, :] = x.astype(BF16)
        return 0
    lax.fori_loop(0, count // TOKS_STEP, body, 0)


def kernel(n, nh, heads, toks, dim,
           q_hbm, k_hbm, v_hbm, c_hbm, no_ref, gq_ref, gk_ref, gv_ref,
           io, st0, st1, qh, kh, vh, ch, raw, gvp, gr,
           own, rs, rp, rx, sp, sx, low, acc, ex_send, ex_recv,
           in_sem, rs_s, rs_r, rp_s, rp_r, rx_s, rx_r, ex_s, ex_r):
    half = heads // 2
    pairs = n // 2
    rows = toks * heads
    width = heads * nh * dim
    seq = lax.axis_index("seq")
    me = lax.axis_index("head")
    pair = seq // 2
    side = seq % 2
    partner = seq + 1 - 2 * side
    own_base = side * half
    oth_base = (1 - side) * half

    landing = (no_ref, gq_ref, io.at[0], io.at[1])
    stages = (st0, st1, gk_ref, gv_ref)
    loads = [
        pltpu.make_async_copy(src, landing[a], in_sem.at[a])
        for a, src in enumerate((k_hbm, v_hbm, q_hbm, c_hbm))
    ]
    loads[0].start()
    loads[1].start()

    barrier = pltpu.get_barrier_semaphore()
    pl.semaphore_signal(barrier, inc=1, device_id={"seq": partner}, device_id_type=MESH)

    @pl.when(pair > 0)
    def _():
        pl.semaphore_signal(barrier, inc=1, device_id={"seq": (seq + n - 2) % n}, device_id_type=MESH)

    @pl.when(pair < pairs - 1)
    def _():
        pl.semaphore_signal(barrier, inc=1, device_id={"seq": (seq + 2) % n}, device_id_type=MESH)

    for d in range(1, nh):
        pl.semaphore_signal(barrier, inc=1, device_id={"head": (me + d) % nh}, device_id_type=MESH)

    def of_head(ref, h):
        return ref.at[pl.ds(h * (toks + 1), toks), :]

    def swap(ph, c):
        return pltpu.make_async_remote_copy(
            src_ref=own.at[ph, oth_base + c], dst_ref=rs.at[ph, c],
            send_sem=rs_s.at[ph, c], recv_sem=rs_r.at[ph, c],
            device_id={"seq": partner}, device_id_type=MESH)

    def chain(ph, c, piece):
        nxt = (seq + 2) % n if ph == 0 else (seq + n - 2) % n
        return pltpu.make_async_remote_copy(
            src_ref=sp.at[ph, c, rows_of(piece)], dst_ref=rp.at[ph, c, rows_of(piece)],
            send_sem=rp_s.at[ph, c, piece], recv_sem=rp_r.at[ph, c, piece],
            device_id={"seq": nxt}, device_id_type=MESH)

    def hand(ph, c):
        return pltpu.make_async_remote_copy(
            src_ref=sx.at[ph, c], dst_ref=rx.at[ph, c],
            send_sem=rx_s.at[ph, c], recv_sem=rx_r.at[ph, c],
            device_id={"seq": partner}, device_id_type=MESH)

    def place(ph):
        return pair if ph == 0 else pairs - 1 - pair

    def rows_of(piece):
        return pl.ds(piece * (dim // PIECES), dim // PIECES)

    def relay(ph, c):
        at = place(ph)
        later = (side == 1) if ph == 0 else (side == 0)
        swap(ph, c).wait_recv()
        for piece in range(PIECES):
            some = rows_of(piece)
            mine = own[ph, own_base + c, some, :]
            theirs = rs[ph, c, some, :]

            @pl.when(at > 0)
            def _():
                chain(ph, c, piece).wait_recv()

            so_far = rp[ph, c, some, :]

            @pl.when(at < pairs - 1)
            def _():
                sp[ph, c, some, :] = so_far + (mine + theirs)
                chain(ph, c, piece).start()

            sx[ph, c, some, :] = so_far + jnp.where(later, 0.0, mine)
            low[ph, own_base + c, some, :] = (so_far + jnp.where(later, theirs, 0.0)).astype(BF16)

    def take(ph, c):
        hand(ph, c).wait_recv()
        low[ph, oth_base + c] = rx[ph, c].astype(BF16)

    batch = 4 if half % 4 == 0 else 1

    def scan(ph, state, ahead, before, unit, finish, after):
        at = place(ph)

        def units_by(c):
            lead = half * at // (2 * (pairs - 1)) + (c + 1) // 2
            return jnp.where(c < 0, 0, jnp.minimum(half, lead))

        defer = jnp.maximum(0, half * (pairs - 1 - at) // (pairs - 1) - half // 4)

        def hands_by(c):
            return jnp.clip(c + 1 - defer, 0, half)

        def takes_by(c):
            return jnp.clip(c - 1 - defer, 0, units_by(c))

        def run(low_end, high_end, step):
            def body(c, _):
                step(c)
                return 0
            lax.fori_loop(low_end, high_end, body, 0)

        def give(c):
            hand(ph, c).start()

        def others(j):
            state([oth_base + j * 2 + i for i in range(2)])
            for i in range(2):
                swap(ph, j * 2 + i).start()

        def owns(j):
            state([own_base + j * batch + i for i in range(batch)])

        def take_one(c):
            take(ph, c)
            finish([own_base + c, oth_base + c])

        def slot(c):
            run(units_by(c - 1), units_by(c), unit)
            relay(ph, c)
            run(hands_by(c - 1), hands_by(c), give)
            run(takes_by(c - 1), takes_by(c), take_one)

        run(0, half // 2, others)
        if ahead is not None:
            ahead()
        run(0, half // batch, owns)
        if before is not None:
            before()
        run(0, half, slot)
        run(hands_by(half - 1), half, give)
        run(units_by(half - 1), half, unit)
        if after is not None:
            after()
        run(takes_by(half - 1), half, take_one)

    for ph in range(2):
        @pl.when(place(ph) == 0)
        def _():
            rp[ph] = jnp.zeros(rp.shape[1:], F32)

    acc[...] = jnp.zeros(acc.shape, F32)
    loads[0].wait()
    loads[2].start()
    loads[3].start()
    all_groups = range(heads // 8)
    by_half = half % 8 == 0

    def spread_half(a, which):
        def of(groups):
            spread(landing[a], stages[a], heads, groups)

        if by_half:
            pl.when(which == 0)(lambda: of(range(half // 8)))
            pl.when(which == 1)(lambda: of(range(half // 8, heads // 8)))
        else:
            of(all_groups)

    spread_half(0, 1 - side)
    loads[1].wait()
    spread_half(1, 1 - side)
    pl.semaphore_wait(
        barrier, nh + jnp.where(pair > 0, 1, 0) + jnp.where(pair < pairs - 1, 1, 0))

    def kv_state(at_once):
        for h in at_once:
            k = of_head(st0, h)[...].astype(BF16)
            v = of_head(st1, h)[...].astype(BF16)
            kh[h] = k
            vh[h] = v
            own[0, h] = dot_tn(k, v)

    def rest_of_keys():
        if by_half:
            spread_half(0, side)
            spread_half(1, side)

    def rest_of_inputs():
        loads[2].wait()
        spread(landing[2], stages[2], heads, all_groups)
        loads[3].wait()
        spread(landing[3], stages[3], heads, all_groups)

    def square(compare):
        return compare(lax.broadcasted_iota(jnp.int32, (CUT, CUT), 1),
                       lax.broadcasted_iota(jnp.int32, (CUT, CUT), 0))

    def keep(mask, x):
        return jnp.where(mask, x, 0.0).astype(BF16)

    def lower(a, b, c):
        mask = square(jnp.less_equal)
        w0 = keep(mask, dot_nt(a[:CUT], b[:CUT]))
        w1 = dot_nt(a[CUT:], b)
        w1 = jnp.concatenate([w1[:, :CUT].astype(BF16), keep(mask, w1[:, CUT:])], axis=1)
        return dot(w0, c[:CUT]), dot(w1, c)

    def upper(a, b, c):
        mask = square(jnp.greater_equal)
        w0 = dot_nt(a[:CUT], b)
        w0 = jnp.concatenate([keep(mask, w0[:, :CUT]), w0[:, CUT:].astype(BF16)], axis=1)
        w1 = keep(mask, dot_nt(a[CUT:], b[CUT:]))
        return dot(w0, c), dot(w1, c[CUT:])

    def local_out(j):
        for h in (own_base + j, oth_base + j):
            q = of_head(gk_ref, h)[...].astype(BF16)
            qh[h] = q
            ch[h] = of_head(gv_ref, h)[...].astype(BF16)
            first, second = lower(q, kh[h], vh[h])
            raw[h, :CUT] = first
            raw[h, CUT:] = second

    blocks = [pl.ds(start, CUT // 2) for start in range(0, toks, CUT // 2)]

    def finish_out(at_once):
        for some in blocks:
            squares, products = acc[0, some, :], acc[1, some, :]
            for h in at_once:
                r = raw[h, some, :] + dot(qh[h, some, :], low[0, h])
                raw[h, some, :] = r
                squares += r * r
                products += ch[h, some, :].astype(F32) * r
            acc[0, some, :] = squares
            acc[1, some, :] = products

    scan(0, kv_state, rest_of_keys, rest_of_inputs, local_out, finish_out, None)

    sq = jnp.sum(acc[0].T, axis=0, keepdims=True)
    inner = jnp.sum(acc[1].T, axis=0, keepdims=True)
    row = lax.broadcasted_iota(jnp.int32, (8, toks), 0)
    ex_send[...] = jnp.where(row < 4, jnp.broadcast_to(sq, (8, toks)), jnp.broadcast_to(inner, (8, toks)))
    peers = [
        pltpu.make_async_remote_copy(
            src_ref=ex_send, dst_ref=ex_recv.at[d - 1],
            send_sem=ex_s.at[d - 1], recv_sem=ex_r.at[d - 1],
            device_id={"head": (me + d) % nh}, device_id_type=MESH)
        for d in range(1, nh)
    ]
    for peer in peers:
        peer.start()
    total = ex_send[...]
    for d, peer in enumerate(peers):
        peer.wait_recv()
        total = total + ex_recv[d]
    inv = lax.rsqrt(total[0:1] / width + EPSILON)
    slope = inv * (total[4:5] / width)
    acc[0] = jnp.broadcast_to(inv, (dim, toks)).T
    acc[1] = jnp.broadcast_to(inv * slope, (dim, toks)).T

    def qg_state(at_once):
        for h in at_once:
            for some in blocks:
                gr[h, some, :] = (acc[0, some, :] * (
                    ch[h, some, :].astype(F32) - raw[h, some, :] * acc[1, some, :])).astype(BF16)
            own[1, h] = dot_tn(qh[h], gr[h])

    def local_grads(j):
        for h in (own_base + j, oth_base + j):
            q, k, v, g = qh[h], kh[h], vh[h], gr[h]
            of_head(st0, h)[...] = raw[h] * acc[0]
            first, second = lower(g, v, k)
            of_head(st1, h)[...] = jnp.concatenate([first, second], axis=0) + dot_nt(g, low[0, h])
            first, second = upper(v, g, q)
            raw[h, :CUT] = first
            raw[h, CUT:] = second
            first, second = upper(k, q, g)
            gvp[h, :CUT] = first
            gvp[h, CUT:] = second

    def finish_grads(at_once):
        for h in at_once:
            of_head(gk_ref, h)[...] = raw[h] + dot_nt(vh[h], low[1, h])
            of_head(gv_ref, h)[...] = gvp[h] + dot(kh[h], low[1, h])

    def early_outs():
        gather(st0, no_ref, heads, 0, toks)
        gather(st1, gq_ref, heads, 0, toks)

    scan(1, qg_state, None, None, local_grads, finish_grads, early_outs)

    for peer in peers:
        peer.wait_send()
    for ph in range(2):
        def drain(c, _, ph=ph):
            swap(ph, c).wait_send()
            hand(ph, c).wait_send()

            @pl.when(place(ph) < pairs - 1)
            def _():
                for piece in range(PIECES):
                    chain(ph, c, piece).wait_send()
            return 0
        lax.fori_loop(0, half, drain, 0)


def write_out(heads, no_ref, gq_ref, gk_ref, gv_ref, no_hbm, gq_hbm, gk_hbm, gv_hbm,
              low_k, low_v, sem, part_sem):
    rows = no_ref.shape[0]
    part = rows // PARTS
    toks = rows // heads
    copies = [
        pltpu.make_async_copy(no_ref, no_hbm, sem.at[0]),
        pltpu.make_async_copy(gq_ref, gq_hbm, sem.at[1]),
    ]
    for copy in copies:
        copy.start()
    for a, (src, low, dst) in enumerate(((gk_ref, low_k, gk_hbm), (gv_ref, low_v, gv_hbm))):
        for j in range(PARTS):
            gather(src, low, heads, j * (toks // PARTS), toks // PARTS)
            at = pl.ds(j * part, part)
            copy = pltpu.make_async_copy(low.at[at], dst.at[at], part_sem.at[a, j])
            copy.start()
            copies.append(copy)
    for copy in copies:
        copy.wait()


def local(n, nh, queries, keys, values, cotangent):
    toks, heads, dim = queries.shape
    rows = toks * heads
    half = heads // 2
    flat = [x.reshape(rows, dim) for x in (queries, keys, values, cotangent)]
    any_spec = pl.BlockSpec(memory_space=pl.ANY)
    sems = pltpu.SemaphoreType.DMA
    per_head = pltpu.VMEM((heads, toks, dim), BF16)
    part = pltpu.VMEM((2, half, dim, dim), F32)
    in_vmem = pl.BlockSpec(memory_space=pltpu.VMEM)
    made = pl.pallas_call(
        functools.partial(kernel, n, nh, heads, toks, dim),
        out_shape=[pltpu.VMEM((rows, dim), BF16)] * 2 + [pltpu.VMEM((rows + heads, dim), F32)] * 2,
        in_specs=[any_spec] * 4,
        out_specs=[in_vmem] * 4,
        scratch_shapes=[
            pltpu.VMEM((2, rows, dim), BF16),
            *[pltpu.VMEM((rows + heads, dim), F32)] * 2,
            *[per_head] * 4,
            *[pltpu.VMEM((heads, toks, dim), F32)] * 2,
            per_head,
            pltpu.VMEM((2, heads, dim, dim), F32),
            *[part] * 5,
            pltpu.VMEM((2, heads, dim, dim), BF16),
            pltpu.VMEM((2, toks, dim), F32),
            pltpu.VMEM((8, toks), F32),
            pltpu.VMEM((nh - 1, 8, toks), F32),
            sems((4,)),
            *[sems((2, half))] * 2,
            *[sems((2, half, PIECES))] * 2,
            *[sems((2, half))] * 2,
            sems((nh - 1,)),
            sems((nh - 1,)),
        ],
        compiler_params=pltpu.CompilerParams(
            collective_id=0, has_side_effects=True, vmem_limit_bytes=44 * 2**20),
        cost_estimate=pl.CostEstimate(
            flops=heads * 10 * toks * toks * dim, bytes_accessed=8 * rows * dim, transcendentals=toks),
    )(*flat)
    outs = pl.pallas_call(
        functools.partial(write_out, heads),
        out_shape=[jax.ShapeDtypeStruct((rows, dim), BF16)] * 4,
        in_specs=[in_vmem] * 4,
        out_specs=[any_spec] * 4,
        scratch_shapes=[*[pltpu.VMEM((rows, dim), BF16)] * 2, sems((2,)), sems((2, PARTS))],
        compiler_params=pltpu.CompilerParams(vmem_limit_bytes=16 * 2**20),
        cost_estimate=pl.CostEstimate(flops=0, bytes_accessed=8 * rows * dim, transcendentals=0),
    )(*made)
    return tuple(x.reshape(toks, heads, dim) for x in outs)


def solution(mesh):
    n, nh = mesh.shape["seq"], mesh.shape["head"]
    spec = P("seq", "head", None)
    return jax.shard_map(
        functools.partial(local, n, nh),
        mesh=mesh,
        in_specs=(spec,) * 4,
        out_specs=(spec,) * 4,
        check_vma=False,
    )
```
